32 devices in a mesh: pairs: 8 (over z, x), rep: 4 (over y, core).
Axes of the slice: x: 2, y: 2, z: 4, core: 2. Of those that a mesh axis runs over, the one named last changes fastest.
Arguments:
- positions: float32 [3, 128, 256], P(None, 'pairs'), may hold values from -1 to 1
- facing: float32 [2, 128, 256], P(None, 'pairs'), may hold values from -3.140625 to 3.140625
- area: float32 [128, 256], P('pairs'), may hold values from 0.00390625 to 0.03125
- emission: float32 [128, 8, 256], P('pairs'), may hold values from 0.1 to 2
- reflect: float32 [128, 8, 256], P('pairs'), may hold values from 0.2 to 0.9
- pair_list: int32 [8, 4, 8, 1, 2], P('pairs', 'rep'), may hold values from -1 to 127, as said below
Outputs:
- radiosity: float32 [128, 8, 256], P('pairs')
The draws below stay inside these ranges and needn't reach their ends.
Inputs may be any that keep to these rules, and one draw needn't show every extreme that they name: `pair_list`: entry [p, r, q, c] is held by the device at pairs index p and rep index r in its slot c toward pairs index q. Its row block lies in p * 16 to (p + 1) * 16 - 1 and its column block in q * 16 to (q + 1) * 16 - 1, or both entries are -1 for an empty slot. Slots toward pairs index 0 are never empty.
All inputs are finite; a program needn't handle non-finite values.
Results may differ from the reference program's by a relative error of at most 0.0003.
Values may be sent and summed in bfloat16 or wider, within the bound.
No kernel may reach another device: no remote copies, remote signals or barrier semaphores. Data moves between devices by JAX's collectives and lax.ppermute only.
A program may use at most 64 MiB of HBM per device.

```python
import math
import jax
import jax.numpy as jnp
from jax import lax

P_SIZE = 256
BANDS = 8
BLK_DEV = 16
CAP = 1
SWEEPS = 2
OWNERS = 8
GROUPS = 4
NBLK = 128


def draw_pair_list(key, part):
    subkeys = jax.random.split(jax.random.fold_in(key, 17), 4)
    grid_shape = (OWNERS, GROUPS, OWNERS, CAP)
    busiest = jax.random.randint(subkeys[0], (OWNERS, 1, 1, 1), 0, GROUPS)
    group_index = jnp.arange(GROUPS, dtype=jnp.int32).reshape(1, GROUPS, 1, 1)
    source_index = jnp.arange(OWNERS, dtype=jnp.int32).reshape(OWNERS, 1, 1, 1)
    target_index = jnp.arange(OWNERS, dtype=jnp.int32).reshape(1, 1, OWNERS, 1)
    threshold = jnp.where(group_index == busiest, 19, 5)
    active = (jax.random.randint(subkeys[1], grid_shape, 0, 20) < threshold) | (target_index == 0)
    row_blocks = source_index * BLK_DEV + jax.random.randint(subkeys[2], grid_shape, 0, BLK_DEV)
    col_blocks = target_index * BLK_DEV + jax.random.randint(subkeys[3], grid_shape, 0, BLK_DEV)
    listed = jnp.stack([jnp.where(active, row_blocks, -1), jnp.where(active, col_blocks, -1)], axis=-1)
    return listed.astype(jnp.int32)


def block_scale(own_key, extent, cuts, smallest, top_value):
    def one(dim, blocks):
        draws = jax.random.uniform(jax.random.fold_in(jax.random.fold_in(own_key, 6), dim), (blocks,), jnp.float32, smallest / len(cuts), top_value / len(cuts))
        return jnp.repeat(jnp.exp(draws), extent[dim] // blocks).reshape((-1,) + (1,) * (len(extent) - dim - 1))

    gain = one(*cuts[0])
    for cut in cuts[1:]:
        gain = gain * one(*cut)
    return gain


def setup_inputs(seed: int = 0) -> dict:
    key_list = jax.random.split(jax.random.key(seed), 7)
    return {
        "positions": jnp.clip(jax.random.uniform(key_list[0], (3, NBLK, P_SIZE), jnp.float32, -1.0, 1.0) * block_scale(key_list[0], (3, NBLK, P_SIZE), ((1, 8),), -0.4, 0.0), -1.0, 1.0),
        "facing": jnp.clip(jax.random.uniform(key_list[1], (2, NBLK, P_SIZE), jnp.float32, -3.140625, 3.140625), -3.140625, 3.140625),
        "area": jnp.clip(jnp.exp(math.log(0.03125) - 2.0794415 * jax.random.uniform(key_list[2], (NBLK, P_SIZE), jnp.float32) ** block_scale(key_list[2], (NBLK, P_SIZE), ((0, 8),), -0.2, 0.2)), 0.00390625, 0.03125),
        "emission": jnp.clip(jnp.exp(math.log(2.0) - 2.9957323 * jax.random.uniform(key_list[3], (NBLK, BANDS, P_SIZE), jnp.float32) ** block_scale(key_list[3], (NBLK, BANDS, P_SIZE), ((0, 8),), -0.2, 0.2)), 0.1, 2.0),
        "reflect": jnp.clip(0.2 + 0.7 * jax.random.uniform(key_list[4], (NBLK, BANDS, P_SIZE), jnp.float32) ** block_scale(key_list[4], (NBLK, BANDS, P_SIZE), ((0, 8),), -0.2, 0.2), 0.2, 0.9),
        "pair_list": draw_pair_list(jax.random.fold_in(key_list[6], 71), 0),
    }


soften = 0.1


def unit_normals(facing):
    azimuth = facing[0]
    elevation = facing[1]
    return jnp.stack([jnp.cos(azimuth) * jnp.cos(elevation), jnp.sin(azimuth) * jnp.cos(elevation), jnp.sin(elevation)], axis=0)


def pack_geometry(positions, facing):
    normals = unit_normals(facing)
    return jnp.transpose(jnp.concatenate([positions, normals], axis=0), (1, 0, 2))


def coupling(row_geom, col_geom):
    offsets = [col_geom[:, axis_id, None, :] - row_geom[:, axis_id, :, None] for axis_id in range(3)]
    spread = offsets[0] * offsets[0] + offsets[1] * offsets[1] + offsets[2] * offsets[2] + soften
    nearside = row_geom[:, 3, :, None] * offsets[0] + row_geom[:, 4, :, None] * offsets[1] + row_geom[:, 5, :, None] * offsets[2]
    farside = col_geom[:, 3, None, :] * offsets[0] + col_geom[:, 4, None, :] * offsets[1] + col_geom[:, 5, None, :] * offsets[2]
    coupled = jnp.maximum(nearside, 0.0) * jnp.maximum(-farside, 0.0) / (jnp.pi * spread * spread)
    return coupled.astype(jnp.bfloat16)


def reference(positions, facing, area, emission, reflect, pair_list):
    geometry = pack_geometry(positions, facing)
    flat_list = pair_list.reshape(-1, 2).astype(jnp.int32)
    per_scan = 64
    extra = (-flat_list.shape[0]) % per_scan
    flat_list = jnp.concatenate([flat_list, jnp.full((extra, 2), -1, jnp.int32)], axis=0)
    active = flat_list[:, 0] >= 0
    row_ids = jnp.where(active, flat_list[:, 0], 0).astype(jnp.int32).reshape(-1, per_scan)
    col_ids = jnp.where(active, flat_list[:, 1], 0).astype(jnp.int32).reshape(-1, per_scan)
    weight_mask = jnp.where(active, 1.0, 0.0).astype(jnp.float32).reshape(-1, per_scan)
    radiosity = emission
    for sweep_index in range(SWEEPS):
        weighted = (area[:, None, :] * radiosity).astype(jnp.bfloat16)

        def accumulate(gathered, pieces):
            rows_now, cols_now, mask_now = pieces
            kernel = coupling(geometry[rows_now], geometry[cols_now]).astype(jnp.float32)
            col_values = weighted[cols_now].astype(jnp.float32)
            row_values = weighted[rows_now].astype(jnp.float32)
            row_terms = jnp.einsum("gij,gbj->gbi", kernel, col_values, precision=lax.Precision.HIGHEST) * mask_now[:, None, None]
            col_terms = jnp.einsum("gij,gbi->gbj", kernel, row_values, precision=lax.Precision.HIGHEST) * mask_now[:, None, None]
            gathered = gathered.at[rows_now].add(row_terms).at[cols_now].add(col_terms)
            return gathered, None

        gathered, unused = lax.scan(accumulate, jnp.zeros(emission.shape, jnp.float32), (row_ids, col_ids, weight_mask))
        radiosity = emission + reflect * gathered
    return radiosity
```

```python
import functools
import math

import jax
import jax.numpy as jnp
from jax import lax
from jax.experimental import pallas as pl
from jax.experimental.pallas import tpu as pltpu
from jax.sharding import PartitionSpec as P

SOFTEN = 0.1
ROWS = 16
CHUNK = 32
KEPT = 32
F32 = jnp.float32
BF16 = jnp.bfloat16
VMEM = pl.BlockSpec(memory_space=pltpu.VMEM)
SMEM = pl.BlockSpec(memory_space=pltpu.SMEM)


def loop(count, body):
    if count <= 16:
        for i in range(count):
            body(i)
    else:
        lax.fori_loop(0, count, lambda i, carry: (body(i), carry)[1], 0)


def read_id(row):
    return jnp.max(row).astype(jnp.int32)


def with_ids(record, first, second):
    rows = lax.broadcasted_iota(jnp.int32, record.shape, 0)
    last = record.shape[0]
    record = jnp.where(rows == last - 2, first.astype(F32), record)
    return jnp.where(rows == last - 1, second.astype(F32), record)


def stage_kernel(bands, copies, held, positions, facing, area, emission, table, sent):
    blocks = area.shape[0]
    azimuth, elevation = facing[0], facing[1]
    level = jnp.cos(elevation)
    table[:, :bands, :] = (area[...][:, None, :] * emission[...]).astype(BF16).astype(F32)
    for axis in range(3):
        table[:, bands + axis, :] = positions[axis]
    table[:, bands + 3, :] = jnp.cos(azimuth) * level
    table[:, bands + 4, :] = jnp.sin(azimuth) * level
    table[:, bands + 5, :] = jnp.sin(elevation)
    table[:, bands + 6, :] = jnp.zeros_like(azimuth)
    table[:, bands + 7, :] = jnp.zeros_like(azimuth)
    owners, capacity = held.shape[0], held.shape[1]

    def one(owner):
        for slot in range(capacity):
            row, col = held[owner, slot, 0], held[owner, slot, 1]
            filled = row >= 0
            row = jnp.where(filled, lax.rem(row, blocks), 0)
            col = jnp.where(filled, lax.rem(col, blocks), -1)
            record = with_ids(table[row], col, row)
            for copy in range(copies):
                sent[owner * copies + copy, slot] = record

    loop(owners, one)


def serve_kernel(bands, table, landed, sent, col_ids):
    def one(slot):
        col = read_id(landed[slot, bands + 6 : bands + 7, :128])
        row = read_id(landed[slot, bands + 7 : bands + 8, :128])
        col_ids[slot] = col
        filled = col >= 0
        sent[slot] = with_ids(
            table[jnp.maximum(col, 0)], jnp.where(filled, row, -1), jnp.where(filled, row, -1)
        )

    loop(landed.shape[0], one)


def form_factors(bands, own, other, write):
    across = other[bands : bands + 8, :].T
    own_rows = [own[bands + k : bands + k + 1, :] for k in range(6)]
    patches = own.shape[1]
    for start in range(0, patches, CHUNK):
        far = [across[start : start + CHUNK, k : k + 1] for k in range(6)]
        d = [far[k] - own_rows[k] for k in range(3)]
        spread = d[0] * d[0] + d[1] * d[1] + d[2] * d[2] + SOFTEN
        near = own_rows[3] * d[0] + own_rows[4] * d[1] + own_rows[5] * d[2]
        away = far[3] * d[0] + far[4] * d[1] + far[5] * d[2]
        value = jnp.maximum(near, 0.0) * jnp.maximum(-away, 0.0) / (math.pi * spread * spread)
        write(start, value.astype(BF16))


def apply_pair(bands, table, landed, kept, scratch, total, slot, own_id):
    own = table[own_id]
    other = landed[slot]

    def write(start, value):
        scratch[pl.ds(start, CHUNK), :] = value

    form_factors(bands, own, other, write)
    matrix = scratch[...]

    def keep():
        kept[slot] = matrix

    if kept.shape[0] == landed.shape[0]:
        keep()
    else:
        pl.when(slot < kept.shape[0])(keep)
    total[own_id] += jnp.dot(other[:bands].astype(BF16), matrix, preferred_element_type=F32)


def column_kernel(bands, table, landed, col_ids, total, kept, scratch):
    total[...] = jnp.zeros_like(total)

    def one(slot, carry):
        own_id = col_ids[slot]

        @pl.when(own_id >= 0)
        def _():
            apply_pair(bands, table, landed, kept, scratch, total, slot, own_id)

        return carry

    lax.fori_loop(0, landed.shape[0], one, 0)


def row_kernel(bands, table, landed, before, total, kept, row_ids, scratch):
    total[...] = before[...]

    def read(slot):
        row_ids[slot] = read_id(landed[slot, bands + 6 : bands + 7, :128])

    loop(landed.shape[0], read)

    def one(slot, carry):
        own_id = row_ids[slot]

        @pl.when(own_id >= 0)
        def _():
            apply_pair(bands, table, landed, kept, scratch, total, slot, own_id)

        return carry

    lax.fori_loop(0, landed.shape[0], one, 0)


def weigh_kernel(area, emission, reflect, mine, theirs, row_ids, col_ids, sent, table):
    radiosity = emission[...] + reflect[...] * (mine[...] + theirs[...])
    table[...] = area[...][:, None, :] * radiosity
    owners, twos = sent.shape[0], sent.shape[1]

    def pick(owner, entry):
        ids = row_ids if entry >= twos else col_ids
        chosen = ids[owner * twos + entry % twos]
        return table[jnp.maximum(chosen, 0)]

    def one(owner):
        for two in range(twos):
            both = jnp.concatenate([pick(owner, 2 * two), pick(owner, 2 * two + 1)], axis=0)
            sent[owner, two] = both.astype(BF16)

    loop(owners, one)


def second_kernel(bands, remade, *refs):
    landed, row_ids, col_ids, row_kept, col_kept = refs[:5]
    total = refs[-2]
    scratch = refs[-1]
    total[...] = jnp.zeros_like(total)
    owners, twos = landed.shape[0], landed.shape[1]

    def one(owner, carry):
        for entry in range(2 * twos):
            ids, kept = (row_ids, row_kept) if entry < twos else (col_ids, col_kept)
            slot = owner * twos + entry % twos
            own_id = ids[slot]

            def add(matrix, own_id=own_id, entry=entry):
                terms = jnp.dot(landed[owner, entry // 2], matrix, preferred_element_type=F32)
                half = (entry % 2) * bands
                total[own_id] += terms[half : half + bands]

            def from_kept(slot=slot, kept=kept, add=add):
                add(kept[slot])

            def from_geometry(slot=slot, own_id=own_id, entry=entry, add=add):
                table = refs[5]
                other = refs[6] if entry < twos else refs[7]

                def write(start, value):
                    scratch[pl.ds(start, CHUNK), :] = value

                form_factors(bands, table[own_id], other[slot], write)
                add(scratch[...])

            if remade:
                held = kept.shape[0]
                pl.when((own_id >= 0) & (slot < held))(from_kept)
                pl.when((own_id >= 0) & (slot >= held))(from_geometry)
            else:
                pl.when(own_id >= 0)(from_kept)
        return carry

    lax.fori_loop(0, owners, one, 0)


def call(kernel, outs, ins, out_specs, scratch=(), flops=0):
    sizes = [math.prod(s.shape) * s.dtype.itemsize for s in outs]
    return pl.pallas_call(
        kernel,
        out_shape=outs,
        in_specs=[SMEM if s else VMEM for s in ins],
        out_specs=out_specs,
        scratch_shapes=scratch,
        compiler_params=pltpu.CompilerParams(vmem_limit_bytes=40 * 1024 * 1024),
        cost_estimate=pl.CostEstimate(flops=flops, bytes_accessed=sum(sizes), transcendentals=0),
    )


def shards(positions, facing, area, emission, reflect, pair_list):
    blocks, bands, patches = emission.shape
    owners = lax.axis_size("pairs")
    reps = lax.axis_size("rep")
    cores = 2 if reps % 2 == 0 else 1
    halves = reps // cores
    held = pair_list[0, 0]
    capacity = held.shape[1]
    per_owner = halves * capacity
    slots = owners * per_owner
    kept_count = min(slots, KEPT)
    rows = bands + 8
    shape = jax.ShapeDtypeStruct
    table_shape = shape((blocks, rows, patches), F32)
    total_shape = shape((blocks, bands, patches), F32)
    kept_shape = shape((kept_count, patches, patches), BF16)
    id_shape = shape((slots,), jnp.int32)
    matrix = pltpu.VMEM((patches, patches), BF16)
    pair_flops = slots * patches * patches * 50

    table, sent = call(
        functools.partial(stage_kernel, bands, halves),
        [table_shape, shape((owners * halves, capacity, rows, patches), F32)],
        [1, 0, 0, 0, 0],
        [VMEM, VMEM],
    )(held, positions, facing, area, emission)
    same_core = [
        [owner * reps + half * cores + core for owner in range(owners) for half in range(halves)]
        for core in range(cores)
    ]
    landed = lax.all_to_all(
        sent,
        ("pairs", "rep"),
        split_axis=0,
        concat_axis=0,
        tiled=True,
        axis_index_groups=same_core,
    )
    col_side = landed.reshape(slots, rows, patches)
    sent, col_ids = call(
        functools.partial(serve_kernel, bands),
        [shape((slots, rows, patches), F32), id_shape],
        [0, 0],
        [VMEM, SMEM],
    )(table, col_side)
    landed = lax.all_to_all(
        sent.reshape(owners, per_owner, rows, patches),
        "pairs",
        split_axis=0,
        concat_axis=0,
        tiled=True,
    )
    row_side = landed.reshape(slots, rows, patches)
    total, col_kept = call(
        functools.partial(column_kernel, bands),
        [total_shape, kept_shape],
        [0, 0, 1],
        [VMEM, VMEM],
        [matrix],
        pair_flops,
    )(table, col_side, col_ids)
    total, row_kept, row_ids = call(
        functools.partial(row_kernel, bands),
        [total_shape, kept_shape, id_shape],
        [0, 0, 0],
        [VMEM, VMEM, SMEM],
        [matrix],
        pair_flops,
    )(table, row_side, total)

    def other_core(x):
        if cores == 1:
            return jnp.zeros_like(x)
        return lax.ppermute(x, "rep", [(i, i ^ 1) for i in range(reps)])

    (sent,) = call(
        weigh_kernel,
        [shape((owners, per_owner, 2 * bands, patches), BF16)],
        [0, 0, 0, 0, 0, 1, 1],
        [VMEM],
        [pltpu.VMEM((blocks, bands, patches), F32)],
    )(area, emission, reflect, total, other_core(total), row_ids, col_ids)
    landed = lax.all_to_all(sent, "pairs", split_axis=0, concat_axis=0, tiled=True)
    remade = kept_count < slots
    extra = [table, row_side, col_side] if remade else []
    (total,) = call(
        functools.partial(second_kernel, bands, remade),
        [total_shape],
        [0, 1, 1, 0, 0] + [0] * len(extra),
        [VMEM],
        [matrix],
        pair_flops,
    )(landed, row_ids, col_ids, row_kept, col_kept, *extra)
    return emission + reflect * (total + other_core(total))


def solution(mesh):
    placed = (
        P(None, "pairs", None),
        P(None, "pairs", None),
        P("pairs", None),
        P("pairs", None, None),
        P("pairs", None, None),
        P("pairs", "rep", None, None, None),
    )
    return jax.shard_map(
        shards, mesh=mesh, in_specs=placed, out_specs=P("pairs", None, None), check_vma=False
    )
```

```python
import functools
import math

import jax
import jax.numpy as jnp
from jax import lax
from jax.experimental import pallas as pl
from jax.experimental.pallas import tpu as pltpu
from jax.sharding import PartitionSpec as P

SOFTEN = 0.1
KEPT = 32
DEPTH = 48
F32 = jnp.float32
BF16 = jnp.bfloat16
VMEM = pl.BlockSpec(memory_space=pltpu.VMEM)
SMEM = pl.BlockSpec(memory_space=pltpu.SMEM)
HBM = pl.BlockSpec(memory_space=pltpu.HBM)


def loop(count, body):
    if count <= 16:
        for i in range(count):
            body(i)
    else:
        lax.fori_loop(0, count, lambda i, carry: (body(i), carry)[1], 0)


def pieces(value, count):
    parts = []
    for _ in range(count):
        part = value.astype(BF16).astype(F32)
        parts.append(part)
        value = value - part
    return parts


def dot_rows(a, b):
    return a[0] * b[0] + a[1] * b[1] + a[2] * b[2]


def with_ids(record, col, row):
    rows = lax.broadcasted_iota(jnp.int32, record.shape, 0)
    lanes = lax.broadcasted_iota(jnp.int32, record.shape, 1)
    ids = jnp.where(lanes < record.shape[1] // 2, col.astype(F32), row.astype(F32))
    return jnp.where(rows == record.shape[0] - 1, ids, record)


def read_ids(record):
    last = record[-8:, :].astype(F32)[7:8, :]
    half = last.shape[1] // 2
    return (
        jnp.max(last[:, :half]).astype(jnp.int32),
        jnp.max(last[:, half:]).astype(jnp.int32),
    )


def stage_kernel(
    bands,
    copies,
    held,
    positions_in,
    facing_in,
    area_in,
    emission_in,
    table,
    geometry,
    sent,
    positions,
    facing,
    area,
    emission,
    done,
):
    moves = [
        pltpu.make_async_copy(src, dst, done.at[i])
        for i, (src, dst) in enumerate(
            (
                (facing_in, facing),
                (positions_in, positions),
                (area_in, area),
                (emission_in, emission),
            )
        )
    ]
    for move in moves:
        move.start()
    blocks = area.shape[0]
    moves[0].wait()
    azimuth, elevation = facing[0], facing[1]
    level = jnp.cos(elevation)
    normal = [jnp.cos(azimuth) * level, jnp.sin(azimuth) * level, jnp.sin(elevation)]
    moves[1].wait()
    place = [positions[axis] for axis in range(3)]
    for axis in range(3):
        geometry[:, axis, :] = place[axis]
        geometry[:, 3 + axis, :] = normal[axis]
        high, middle, low = pieces(place[axis], 3)
        table[:, bands + axis, :] = high
        table[:, bands + 8 + axis, :] = middle
        table[:, bands + (6, 7, 14)[axis], :] = low
        high, low = pieces(normal[axis], 2)
        table[:, bands + 3 + axis, :] = high
        table[:, bands + 11 + axis, :] = low
    table[:, bands + 15, :] = jnp.zeros_like(azimuth)
    geometry[:, 6, :] = dot_rows(place, normal)
    geometry[:, 7, :] = dot_rows(place, place)
    moves[2].wait()
    moves[3].wait()
    table[:, :bands, :] = (area[...][:, None, :] * emission[...]).astype(BF16).astype(F32)
    capacity, _, owners = held.shape

    def one(owner):
        for slot in range(capacity):
            row, col = held[slot, 0, owner], held[slot, 1, owner]
            filled = row >= 0
            row = jnp.where(filled, lax.rem(row, blocks), 0)
            col = jnp.where(filled, lax.rem(col, blocks), -1)
            record = with_ids(table[row], col, row).astype(BF16)
            for copy in range(copies):
                sent[owner * copies + copy, slot] = record

    loop(owners, one)


def own_kernel(
    geometry, area_in, emission_in, reflect_in, out, area, emission, reflect, factors, done
):
    moves = [
        pltpu.make_async_copy(src, dst, done.at[i])
        for i, (src, dst) in enumerate(
            ((area_in, area), (emission_in, emission), (reflect_in, reflect))
        )
    ]
    for move in moves:
        move.start()

    def one(block):
        tile = geometry[block]
        patches = tile.shape[1]
        row = [tile[k : k + 1, :] for k in range(8)]
        none = jnp.zeros_like(row[0])
        unit = jnp.ones_like(none)

        def stack(*rows):
            return jnp.concatenate(rows, axis=0)

        n = list(zip(*[pieces(row[3 + k] * (1.0 / math.pi), 3) for k in range(3)]))
        c = pieces(row[6] * (-1.0 / math.pi), 3)
        near = stack(
            *n[0], none, none, none, n[0][0], n[0][1],
            *n[0], none, none, none, n[0][2], none,
            *n[1], none, none, none, none, none,
            *n[1], none, none, none, none, none,
            *n[2], none, none, none, c[0], c[1],
            none, none, none, none, none, none, c[2], none,
        )
        p = list(zip(*[pieces(row[k], 3) for k in range(3)]))
        away = stack(
            none, none, none, *p[0], none, none,
            none, none, none, *p[0], none, none,
            none, none, none, *p[1], none, none,
            none, none, none, *p[1], none, none,
            none, none, none, *p[2], none, none,
            -unit, -unit, -unit, none, none, none, none, none,
        )
        m = [[-2.0 * v for v in part] for part in p]
        e = pieces(row[7] + SOFTEN, 3)
        spread = stack(
            *m[0], none, none, none, m[0][0], m[0][1],
            *m[0], none, none, none, m[0][2], none,
            *m[1], none, none, none, none, none,
            *m[1], none, none, none, none, none,
            *m[2], none, none, none, e[0], e[1],
            none, none, none, unit, unit, unit, e[2], none,
        )
        factors[block, :, 0:patches] = near.astype(BF16)
        factors[block, :, patches : 2 * patches] = away.astype(BF16)
        factors[block, :, 2 * patches :] = spread.astype(BF16)

    lax.fori_loop(0, geometry.shape[0], lambda i, carry: (one(i), carry)[1], 0, unroll=2)
    save = pltpu.make_async_copy(factors, out, done.at[3])
    save.start()
    for move in moves:
        move.wait()
    save.wait()


def serve_kernel(table, landed, sent, col_ids):
    def one(slot):
        col, row = read_ids(landed[slot])
        col_ids[slot] = col
        filled = col >= 0
        row = jnp.where(filled, row, -1)
        sent[slot] = with_ids(table[jnp.maximum(col, 0)], row, row).astype(BF16)

    loop(landed.shape[0], one)


def other_sides(bands, landed, wide, sides):
    slots = landed.shape[0]

    def widen(slot):
        wide[slot] = landed[slot].astype(F32)

    loop(slots, widen)

    def row(index):
        return wide[:, bands + index, :]

    place = [row(k) + row(8 + k) + row((6, 7, 14)[k]) for k in range(3)]
    normal = [row(3 + k) + row(11 + k) for k in range(3)]
    constants = pieces(dot_rows(place, normal), 3) + pieces(dot_rows(place, place), 3)
    for k, value in enumerate(constants):
        wide[:, k, :] = value
    wide[:, 6, :] = jnp.ones_like(place[0])
    wide[:, 7, :] = jnp.zeros_like(place[0])

    def side(slot):
        last = wide[slot, :8, :]
        first = wide[slot, 8:16, :]
        second = wide[slot, 16:24, :]
        rows = lax.broadcasted_iota(jnp.int32, first.shape, 0)
        with_ones = jnp.where(rows < 6, first, 1.0)
        sides[slot] = jnp.concatenate(
            [first, second, first, second, with_ones, last], axis=0
        ).astype(BF16)

    loop(slots, side)


def form_factors(side, factors):
    patches = side.shape[1]
    parts = lax.dot_general(
        side, factors, (((0,), (0,)), ((), ())), preferred_element_type=F32
    )
    near = parts[:, :patches]
    away = parts[:, patches : 2 * patches]
    spread = parts[:, 2 * patches :]
    inverse = pl.reciprocal(spread, approx=True)
    inverse = inverse * (2.0 - spread * inverse)
    value = jnp.maximum(near, 0.0) * jnp.maximum(away, 0.0) * (inverse * inverse)
    return value.astype(BF16)


def first_sweep(bands, factors, landed, ids, sides, total, kept):
    slots = landed.shape[0]

    def one(slot):
        own_id = ids[slot]
        own = jnp.maximum(own_id, 0)
        matrix = form_factors(sides[slot], factors[own])

        def keep():
            kept[slot] = matrix

        if kept.shape[0] == slots:
            keep()
        else:
            pl.when(slot < kept.shape[0])(keep)
        weights = landed[slot].astype(F32)[:bands].astype(BF16)
        terms = jnp.dot(weights, matrix, preferred_element_type=F32)
        total[own] += jnp.where(own_id >= 0, terms, 0.0)

    loop(slots, one)


def column_kernel(bands, factors_in, landed, col_ids, total, kept, sides, wide, factors, done):
    load = pltpu.make_async_copy(factors_in, factors, done.at[0])
    load.start()
    total[...] = jnp.zeros_like(total)
    other_sides(bands, landed, wide, sides)
    load.wait()
    first_sweep(bands, factors, landed, col_ids, sides, total, kept)


def row_kernel(
    bands, factors_in, landed, before, total, kept, row_ids, sides, wide, factors, done
):
    load = pltpu.make_async_copy(factors_in, factors, done.at[0])
    load.start()
    total[...] = before[...]

    def read(slot):
        row_ids[slot] = read_ids(landed[slot])[0]

    loop(landed.shape[0], read)
    other_sides(bands, landed, wide, sides)
    load.wait()
    first_sweep(bands, factors, landed, row_ids, sides, total, kept)


def weigh_kernel(area, emission, reflect, mine, theirs, row_ids, col_ids, sent, table):
    radiosity = emission[...] + reflect[...] * (mine[...] + theirs[...])
    table[...] = area[...][:, None, :] * radiosity
    owners, twos = sent.shape[0], sent.shape[1]

    def pick(owner, entry):
        ids = row_ids if entry >= twos else col_ids
        chosen = ids[owner * twos + entry % twos]
        return table[jnp.maximum(chosen, 0)]

    def one(owner):
        for two in range(twos):
            both = jnp.concatenate([pick(owner, 2 * two), pick(owner, 2 * two + 1)], axis=0)
            sent[owner, two] = both.astype(BF16)

    loop(owners, one)


def second_kernel(bands, remade, *refs):
    landed, row_ids, col_ids, row_kept, col_kept = refs[:5]
    total = refs[-1]
    total[...] = jnp.zeros_like(total)
    owners, twos = landed.shape[0], landed.shape[1]

    def one(owner):
        for entry in range(2 * twos):
            own_side = entry < twos
            ids, kept = (row_ids, row_kept) if own_side else (col_ids, col_kept)
            slot = owner * twos + entry % twos
            own_id = ids[slot]
            own = jnp.maximum(own_id, 0)
            weights = landed[owner, entry // 2]
            half = (entry % 2) * bands

            def add(matrix, own_id=own_id, own=own, weights=weights, half=half):
                terms = jnp.dot(weights, matrix, preferred_element_type=F32)
                total[own] += jnp.where(own_id >= 0, terms[half : half + bands], 0.0)

            if not remade:
                add(kept[slot])
                continue

            def from_kept(slot=slot, kept=kept, add=add):
                add(kept[slot])

            def from_sides(slot=slot, own=own, own_side=own_side, add=add):
                sides = refs[6] if own_side else refs[7]
                add(form_factors(sides[slot], refs[5][own]))

            held = kept.shape[0]
            pl.when((own_id >= 0) & (slot < held))(from_kept)
            pl.when((own_id >= 0) & (slot >= held))(from_sides)

    loop(owners, one)


def in_hbm(x):
    return pltpu.with_memory_space_constraint(x, pltpu.HBM)


def call(kernel, outs, ins, out_specs, scratch=(), flops=0):
    sizes = [math.prod(s.shape) * s.dtype.itemsize for s in outs]
    held = [math.prod(s.shape) * s.dtype.itemsize for s in scratch if s.dtype in (F32, BF16)]
    room = 2 * sum(sizes) + sum(held) + 8 * 1024 * 1024
    return pl.pallas_call(
        kernel,
        out_shape=[
            pltpu.VMEM(s.shape, s.dtype) if spec is VMEM else s for s, spec in zip(outs, out_specs)
        ],
        in_specs=ins,
        out_specs=out_specs,
        scratch_shapes=scratch,
        compiler_params=pltpu.CompilerParams(vmem_limit_bytes=room),
        cost_estimate=pl.CostEstimate(flops=flops, bytes_accessed=sum(sizes), transcendentals=0),
    )


def shards(positions, facing, area, emission, reflect, pair_list):
    blocks, bands, patches = emission.shape
    owners = lax.axis_size("pairs")
    reps = lax.axis_size("rep")
    cores = 2 if reps % 2 == 0 else 1
    halves = reps // cores
    held = jnp.transpose(pair_list[0, 0], (1, 2, 0))
    capacity = held.shape[0]
    per_owner = halves * capacity
    slots = owners * per_owner
    kept_count = min(slots, KEPT)
    remade = kept_count < slots
    rows = bands + 16
    shape = jax.ShapeDtypeStruct
    total_shape = shape((blocks, bands, patches), F32)
    kept_shape = shape((kept_count, patches, patches), BF16)
    id_shape = shape((slots,), jnp.int32)
    wide = pltpu.VMEM((slots, rows, patches), F32)
    pair_flops = slots * patches * patches * 50

    table, geometry, sent = call(
        functools.partial(stage_kernel, bands, halves),
        [
            shape((blocks, rows, patches), F32),
            shape((blocks, 8, patches), F32),
            shape((owners * halves, capacity, rows, patches), BF16),
        ],
        [SMEM, HBM, HBM, HBM, HBM],
        [VMEM, VMEM, VMEM],
        [
            pltpu.VMEM(positions.shape, F32),
            pltpu.VMEM(facing.shape, F32),
            pltpu.VMEM(area.shape, F32),
            pltpu.VMEM(emission.shape, F32),
            pltpu.SemaphoreType.DMA((4,)),
        ],
    )(held, in_hbm(positions), in_hbm(facing), in_hbm(area), in_hbm(emission))
    same_core = [
        [owner * reps + half * cores + core for owner in range(owners) for half in range(halves)]
        for core in range(cores)
    ]
    landed = lax.all_to_all(
        sent,
        ("pairs", "rep"),
        split_axis=0,
        concat_axis=0,
        tiled=True,
        axis_index_groups=same_core,
    )
    factors_scratch = pltpu.VMEM((blocks, DEPTH, 3 * patches), BF16)
    factors, area, emission, reflect = call(
        own_kernel,
        [
            pltpu.HBM(factors_scratch.shape, BF16),
            shape(area.shape, F32),
            total_shape,
            total_shape,
        ],
        [VMEM, HBM, HBM, HBM],
        [HBM, VMEM, VMEM, VMEM],
        [factors_scratch, pltpu.SemaphoreType.DMA((4,))],
        pair_flops,
    )(geometry, in_hbm(area), in_hbm(emission), in_hbm(reflect))
    col_side = landed.reshape(slots, rows, patches)
    sent, col_ids = call(
        serve_kernel, [shape((slots, rows, patches), BF16), id_shape], [VMEM, VMEM], [VMEM, SMEM]
    )(table, col_side)
    landed = lax.all_to_all(
        sent.reshape(owners, per_owner, rows, patches),
        "pairs",
        split_axis=0,
        concat_axis=0,
        tiled=True,
    )
    row_side = landed.reshape(slots, rows, patches)
    sides_shape = shape((slots, DEPTH, patches), BF16)
    sides = pltpu.VMEM(sides_shape.shape, BF16)
    kept_sides = [sides_shape] if remade else []
    own_sides = [] if remade else [sides]
    total, col_kept, *col_sides = call(
        functools.partial(column_kernel, bands),
        [total_shape, kept_shape] + kept_sides,
        [HBM, VMEM, SMEM],
        [VMEM, VMEM] + [VMEM] * len(kept_sides),
        own_sides + [wide, factors_scratch, pltpu.SemaphoreType.DMA((1,))],
        pair_flops,
    )(in_hbm(factors), col_side, col_ids)
    total, row_kept, row_ids, *row_sides = call(
        functools.partial(row_kernel, bands),
        [total_shape, kept_shape, id_shape] + kept_sides,
        [HBM, VMEM, VMEM],
        [VMEM, VMEM, SMEM] + [VMEM] * len(kept_sides),
        own_sides + [wide, factors_scratch, pltpu.SemaphoreType.DMA((1,))],
        pair_flops,
    )(in_hbm(factors), row_side, total)

    def other_core(x):
        if cores == 1:
            return jnp.zeros_like(x)
        return lax.ppermute(x, "rep", [(i, i ^ 1) for i in range(reps)])

    (sent,) = call(
        weigh_kernel,
        [shape((owners, per_owner, 2 * bands, patches), BF16)],
        [VMEM] * 5 + [SMEM, SMEM],
        [VMEM],
        [pltpu.VMEM((blocks, bands, patches), F32)],
    )(area, emission, reflect, total, other_core(total), row_ids, col_ids)
    landed = lax.all_to_all(sent, "pairs", split_axis=0, concat_axis=0, tiled=True)
    extra = [factors, *row_sides, *col_sides] if remade else []
    (total,) = call(
        functools.partial(second_kernel, bands, remade),
        [total_shape],
        [VMEM, SMEM, SMEM, VMEM, VMEM] + [VMEM] * len(extra),
        [VMEM],
        (),
        pair_flops,
    )(landed, row_ids, col_ids, row_kept, col_kept, *extra)
    return emission + reflect * (total + other_core(total))


def solution(mesh):
    placed = (
        P(None, "pairs", None),
        P(None, "pairs", None),
        P("pairs", None),
        P("pairs", None, None),
        P("pairs", None, None),
        P("pairs", "rep", None, None, None),
    )
    return jax.shard_map(
        shards, mesh=mesh, in_specs=placed, out_specs=P("pairs", None, None), check_vma=False
    )
```

```python
import functools
import math

import jax
import jax.numpy as jnp
from jax import lax
from jax.experimental import pallas as pl
from jax.experimental.pallas import tpu as pltpu
from jax.sharding import PartitionSpec as P

SOFTEN = 0.1
KEPT = 32
DEPTH = 48
F32 = jnp.float32
BF16 = jnp.bfloat16
VMEM = pl.BlockSpec(memory_space=pltpu.VMEM)
SMEM = pl.BlockSpec(memory_space=pltpu.SMEM)
HBM = pl.BlockSpec(memory_space=pltpu.HBM)


def loop(count, body):
    if count <= 16:
        for i in range(count):
            body(i)
    else:
        lax.fori_loop(0, count, lambda i, carry: (body(i), carry)[1], 0)


def pieces(value, count):
    parts = []
    for _ in range(count):
        part = value.astype(BF16).astype(F32)
        parts.append(part)
        value = value - part
    return parts


def dot_rows(a, b):
    return a[0] * b[0] + a[1] * b[1] + a[2] * b[2]


def with_ids(record, ids):
    rows = lax.broadcasted_iota(jnp.int32, record.shape, 0)
    return jnp.where(rows == record.shape[0] - 1, ids, record)


def read_id(ids):
    return ids[:, :128][0, 0].astype(jnp.int32)


def stage_kernel(
    bands,
    held_in,
    positions_in,
    facing_in,
    area_in,
    emission_in,
    reflect_in,
    table,
    geometry,
    sent,
    area,
    emission,
    reflect,
    held,
    positions,
    facing,
    done,
):
    moves = [
        pltpu.make_async_copy(src, dst, done.at[i])
        for i, (src, dst) in enumerate(
            (
                (facing_in, facing),
                (positions_in, positions),
                (area_in, area),
                (emission_in, emission),
                (held_in, held),
                (reflect_in, reflect),
            )
        )
    ]
    for move in moves:
        move.start()
    blocks, patches = area.shape
    capacity, _, owners = held.shape
    moves[0].wait()
    azimuth, elevation = facing[0], facing[1]
    level = jnp.cos(elevation)
    normal = [jnp.cos(azimuth) * level, jnp.sin(azimuth) * level, jnp.sin(elevation)]
    moves[1].wait()
    place = [positions[axis] for axis in range(3)]
    for axis in range(3):
        geometry[:, axis, :] = place[axis]
        geometry[:, 3 + axis, :] = normal[axis]
        high, middle, low = pieces(place[axis], 3)
        table[:, bands + axis, :] = high
        table[:, bands + 8 + axis, :] = middle
        table[:, bands + (6, 7, 14)[axis], :] = low
        high, low = pieces(normal[axis], 2)
        table[:, bands + 3 + axis, :] = high
        table[:, bands + 11 + axis, :] = low
    table[:, bands + 15, :] = jnp.zeros_like(azimuth)
    geometry[:, 6, :] = dot_rows(place, normal)
    geometry[:, 7, :] = dot_rows(place, place)
    moves[4].wait()
    lanes = lax.broadcasted_iota(jnp.int32, (1, patches), 1)
    moves[2].wait()
    moves[3].wait()
    table[:, :bands, :] = (area[...][:, None, :] * emission[...]).astype(BF16).astype(F32)

    def one(owner):
        for slot in range(capacity):
            row, col = held[slot, 0, owner], held[slot, 1, owner]
            filled = row >= 0
            row = jnp.where(filled, lax.rem(row, blocks), -1)
            col = jnp.where(filled, lax.rem(col, blocks), -1)
            ids = jnp.where(lanes < patches // 2, col.astype(F32), row.astype(F32))
            sent[owner, slot] = with_ids(table[jnp.maximum(row, 0)], ids).astype(BF16)

    loop(owners, one)
    moves[5].wait()


def serve_kernel(copies, table, landed, sent, mirror):
    capacity = sent.shape[1]

    def one(slot):
        record = landed[slot].astype(F32)
        mirror[slot] = record[-16:].astype(BF16)
        ids = record[-1:]
        row = ids[:, ids.shape[1] // 2 :]
        answer = table[jnp.maximum(read_id(ids), 0)]
        answer = with_ids(answer, jnp.concatenate([row, row], axis=1)).astype(BF16)
        for copy in range(copies):
            sent[slot // capacity * copies + copy, slot % capacity] = answer

    loop(landed.shape[0], one)


def own_factors(tile):
    row = [tile[k : k + 1, :] for k in range(8)]
    none = jnp.zeros_like(row[0])
    unit = jnp.ones_like(none)

    def stack(*rows):
        return jnp.concatenate(rows, axis=0)

    n = list(zip(*[pieces(row[3 + k] * (1.0 / math.pi), 3) for k in range(3)]))
    c = pieces(row[6] * (-1.0 / math.pi), 3)
    near = stack(
        *n[0], none, none, none, n[0][0], n[0][1],
        *n[0], none, none, none, n[0][2], none,
        *n[1], none, none, none, none, none,
        *n[1], none, none, none, none, none,
        *n[2], none, none, none, c[0], c[1],
        none, none, none, none, none, none, c[2], none,
    )
    p = list(zip(*[pieces(row[k], 3) for k in range(3)]))
    away = stack(
        none, none, none, *p[0], none, none,
        none, none, none, *p[0], none, none,
        none, none, none, *p[1], none, none,
        none, none, none, *p[1], none, none,
        none, none, none, *p[2], none, none,
        -unit, -unit, -unit, none, none, none, none, none,
    )
    m = [[-2.0 * v for v in part] for part in p]
    e = pieces(row[7] + SOFTEN, 3)
    spread = stack(
        *m[0], none, none, none, m[0][0], m[0][1],
        *m[0], none, none, none, m[0][2], none,
        *m[1], none, none, none, none, none,
        *m[1], none, none, none, none, none,
        *m[2], none, none, none, e[0], e[1],
        none, none, none, unit, unit, unit, e[2], none,
    )
    return jnp.concatenate([near, away, spread], axis=1).astype(BF16)


def other_sides(bands, wide, sides):
    slots = wide.shape[0]

    def row(index):
        return wide[:, bands + index, :]

    place = [row(k) + row(8 + k) + row((6, 7, 14)[k]) for k in range(3)]
    normal = [row(3 + k) + row(11 + k) for k in range(3)]
    constants = pieces(dot_rows(place, normal), 3) + pieces(dot_rows(place, place), 3)
    constants += [jnp.ones_like(place[0]), jnp.zeros_like(place[0])]
    rows = lax.broadcasted_iota(jnp.int32, (8, wide.shape[2]), 0)
    for k, value in enumerate(constants):
        wide[:, bands + 16 + k, :] = value

    def side(slot):
        first = wide[slot, bands : bands + 8, :]
        second = wide[slot, bands + 8 : bands + 16, :]
        last = wide[slot, bands + 16 : bands + 24, :]
        with_ones = jnp.where(rows < 6, first, 1.0)
        sides[slot] = jnp.concatenate(
            [first, second, first, second, with_ones, last], axis=0
        ).astype(BF16)

    loop(slots, side)


def form_factors(side, factors):
    patches = side.shape[1]
    parts = lax.dot_general(
        side, factors, (((0,), (0,)), ((), ())), preferred_element_type=F32
    )
    near = parts[:, :patches]
    away = parts[:, patches : 2 * patches]
    spread = parts[:, 2 * patches :]
    inverse = pltpu.reciprocal(spread, approx=True)
    inverse = inverse * (2.0 - spread * inverse)
    value = jnp.maximum(near, 0.0) * jnp.maximum(away, 0.0) * (inverse * inverse)
    return value.astype(BF16)


def build_matrices(bands, geometry, landed, order, ids, kept, sides, wide):
    def widen(slot):
        record = landed[order(slot)].astype(F32)
        wide[slot, bands + 16 - record.shape[0] : bands + 16, :] = record
        ids[slot] = read_id(record[-1:])

    loop(wide.shape[0], widen)
    other_sides(bands, wide, sides)

    def build(slot):
        return form_factors(sides[slot], own_factors(geometry[jnp.maximum(ids[slot], 0)]))

    def keep(slot):
        kept[slot] = build(slot)

    loop(kept.shape[0], keep)
    return build


def first_sweep(bands, geometry, landed, order, ids, total, kept, sides, wide):
    build = build_matrices(bands, geometry, landed, order, ids, kept, sides, wide)

    def add(slot, matrix):
        own_id = ids[slot]
        weights = wide[slot, :bands, :].astype(BF16)
        terms = jnp.dot(weights, matrix, preferred_element_type=F32)
        total[jnp.maximum(own_id, 0)] += jnp.where(own_id >= 0, terms, 0.0)

    def add_kept(slot):
        add(slot, kept[slot])

    def add_built(slot):
        add(slot, build(slot))

    held, slots = kept.shape[0], wide.shape[0]
    loop(held, add_kept)
    if held < slots:
        lax.fori_loop(held, slots, lambda i, carry: (add_built(i), carry)[1], 0)


def column_kernel(bands, geometry, landed, total, kept, ids, sides, wide):
    total[...] = jnp.zeros_like(total)
    first_sweep(bands, geometry, landed, lambda i: i, ids, total, kept, sides, wide)


def other_column_kernel(bands, geometry, landed, after, kept, ids, sides, wide):
    build_matrices(bands, geometry, landed, lambda i: i, ids, kept, sides, wide)


def row_kernel(bands, cores, halves, geometry, landed, before, total, kept, ids, sides, wide):
    capacity = landed.shape[0] // (lax.axis_size("pairs") * halves)
    here = lax.axis_index("rep") // cores

    def order(slot):
        owner, back, entry = slot // (halves * capacity), slot // capacity % halves, slot % capacity
        half = lax.rem(here + (halves - back), halves)
        return (owner * halves + half) * capacity + entry

    total[...] = before[...]
    first_sweep(bands, geometry, landed, order, ids, total, kept, sides, wide)


def add_kernel(parts, *refs):
    total = refs[0][...]
    for part in refs[1:parts]:
        total = total + part[...]
    refs[-1][...] = total


def weigh_kernel(halves, area, emission, reflect, mine, theirs, row_ids, *refs):
    col_ids = refs[:halves]
    sent, table = refs[halves:]
    radiosity = emission[...] + reflect[...] * (mine[...] + theirs[...])
    table[...] = area[...][:, None, :] * radiosity
    owners, twos = sent.shape[0], sent.shape[1]
    capacity = twos // halves

    def pick(owner, entry):
        if entry < twos:
            chosen = col_ids[entry // capacity][owner * capacity + entry % capacity]
        else:
            chosen = row_ids[owner * twos + entry - twos]
        return table[jnp.maximum(chosen, 0)]

    def one(owner):
        for two in range(twos):
            both = jnp.concatenate([pick(owner, 2 * two), pick(owner, 2 * two + 1)], axis=0)
            sent[owner, two] = both.astype(BF16)

    loop(owners, one)


def second_kernel(bands, halves, remade, landed, row_ids, row_kept, *refs):
    col_ids, col_kept = refs[:halves], refs[halves : 2 * halves]
    total = refs[-1]
    if remade:
        geometry, row_sides, *col_sides = refs[2 * halves : -1]
    total[...] = jnp.zeros_like(total)
    owners, twos = landed.shape[0], landed.shape[1]
    capacity = twos // halves

    def one(owner):
        for entry in range(2 * twos):
            part = entry // capacity - halves
            if entry < twos:
                ids, kept, slot = row_ids, row_kept, owner * twos + entry
            else:
                ids, kept = col_ids[part], col_kept[part]
                slot = owner * capacity + entry % capacity
            own_id = ids[slot]
            own = jnp.maximum(own_id, 0)
            weights = landed[owner, entry // 2]
            half = (entry % 2) * bands

            def add(matrix, own_id=own_id, own=own, weights=weights, half=half):
                terms = jnp.dot(weights, matrix, preferred_element_type=F32)
                total[own] += jnp.where(own_id >= 0, terms[half : half + bands], 0.0)

            if not remade:
                add(kept[slot])
                continue
            sides = row_sides if entry < twos else col_sides[part]

            def from_kept(slot=slot, kept=kept, add=add):
                add(kept[slot])

            def from_sides(slot=slot, own=own, sides=sides, add=add):
                add(form_factors(sides[slot], own_factors(geometry[own])))

            held = kept.shape[0]
            pl.when((own_id >= 0) & (slot < held))(from_kept)
            pl.when((own_id >= 0) & (slot >= held))(from_sides)

    loop(owners, one)


def in_hbm(x):
    return pltpu.with_memory_space_constraint(x, pltpu.HBM)


def in_smem(x):
    return pltpu.with_memory_space_constraint(x, pltpu.SMEM)


def call(kernel, outs, ins, out_specs, scratch=(), flops=0):
    sizes = [math.prod(s.shape) * s.dtype.itemsize for s in outs]
    held = [math.prod(s.shape) * s.dtype.itemsize for s in scratch if s.dtype in (F32, BF16)]
    room = 2 * sum(sizes) + sum(held) + 8 * 1024 * 1024
    return pl.pallas_call(
        kernel,
        out_shape=[
            spec.memory_space(s.shape, s.dtype) for s, spec in zip(outs, out_specs)
        ],
        in_specs=ins,
        out_specs=out_specs,
        scratch_shapes=scratch,
        compiler_params=pltpu.CompilerParams(vmem_limit_bytes=room),
        cost_estimate=pl.CostEstimate(flops=flops, bytes_accessed=sum(sizes), transcendentals=0),
    )


def shards(positions, facing, area, emission, reflect, pair_list):
    blocks, bands, patches = emission.shape
    owners = lax.axis_size("pairs")
    reps = lax.axis_size("rep")
    cores = 2 if reps % 2 == 0 else 1
    halves = reps // cores
    held = jnp.transpose(pair_list[0, 0], (1, 2, 0))
    capacity = held.shape[0]
    per_owner = halves * capacity
    slots = owners * per_owner
    near_slots = owners * capacity
    remade = slots > KEPT
    rows = bands + 16
    shape = jax.ShapeDtypeStruct
    total_shape = shape((blocks, bands, patches), F32)
    pair_flops = slots * patches * patches * 50

    def kept_of(count):
        return shape((min(count, KEPT), patches, patches), BF16)

    def sweep_room(count):
        sides = shape((count, DEPTH, patches), BF16)
        wide = pltpu.VMEM((count, rows + 8, patches), F32)
        if remade:
            return [sides], [wide]
        return [], [pltpu.VMEM(sides.shape, BF16), wide]

    table, geometry, sent, area, emission, reflect = call(
        functools.partial(stage_kernel, bands),
        [
            shape((blocks, rows, patches), F32),
            shape((blocks, 8, patches), F32),
            shape((owners, capacity, rows, patches), BF16),
            shape(area.shape, F32),
            total_shape,
            total_shape,
        ],
        [HBM] * 6,
        [VMEM] * 6,
        [
            pltpu.SMEM(held.shape, jnp.int32),
            pltpu.VMEM(positions.shape, F32),
            pltpu.VMEM(facing.shape, F32),
            pltpu.SemaphoreType.DMA((6,)),
        ],
    )(*[in_hbm(x) for x in (held, positions, facing, area, emission, reflect)])
    landed = lax.all_to_all(sent, "pairs", split_axis=0, concat_axis=0, tiled=True)
    col_side = landed.reshape(near_slots, rows, patches)
    sent, mirror = call(
        functools.partial(serve_kernel, halves),
        [
            shape((owners * halves, capacity, rows, patches), BF16),
            shape((near_slots, 16, patches), BF16),
        ],
        [VMEM, VMEM],
        [VMEM, VMEM],
    )(table, col_side)
    same_core = [
        [owner * reps + half * cores + core for owner in range(owners) for half in range(halves)]
        for core in range(cores)
    ]
    landed = lax.all_to_all(
        sent,
        ("pairs", "rep"),
        split_axis=0,
        concat_axis=0,
        tiled=True,
        axis_index_groups=same_core,
    )
    row_side = landed.reshape(slots, rows, patches)

    def other_halves(x):
        return [
            lax.ppermute(x, "rep", [(i, (i + back * cores) % reps) for i in range(reps)])
            for back in range(1, halves)
        ]

    mirrors = other_halves(mirror)
    near_ids = shape((near_slots,), jnp.int32)
    outs, room = sweep_room(near_slots)
    col_total, kept, ids, *sides = call(
        functools.partial(column_kernel, bands),
        [total_shape, kept_of(near_slots), near_ids] + outs,
        [VMEM, VMEM],
        [VMEM, VMEM, SMEM] + [VMEM] * len(outs),
        room,
        pair_flops // halves,
    )(geometry, col_side)
    col_ids, col_kept, col_sides = [in_smem(ids)], [kept], [*sides]
    far_totals = other_halves(col_total)
    outs, room = sweep_room(slots)
    total, row_kept, row_ids, *row_sides = call(
        functools.partial(row_kernel, bands, cores, halves),
        [total_shape, kept_of(slots), shape((slots,), jnp.int32)] + outs,
        [VMEM, VMEM, VMEM],
        [VMEM, VMEM, SMEM] + [VMEM] * len(outs),
        room,
        pair_flops,
    )(geometry, row_side, col_total)
    row_ids = in_smem(row_ids)
    if far_totals:
        (total,) = call(
            functools.partial(add_kernel, halves),
            [total_shape],
            [VMEM] * (halves + len(mirrors)),
            [VMEM],
        )(total, *far_totals, *mirrors)
    outs, room = sweep_room(near_slots)
    for mirror in mirrors:
        kept, ids, *sides = call(
            functools.partial(other_column_kernel, bands),
            [kept_of(near_slots), near_ids] + outs,
            [VMEM, VMEM, VMEM],
            [VMEM, SMEM] + [VMEM] * len(outs),
            room,
            pair_flops // halves,
        )(geometry, mirror, total)
        col_ids.append(in_smem(ids))
        col_kept.append(kept)
        col_sides.extend(sides)

    def other_core(x):
        if cores == 1:
            return jnp.zeros_like(x)
        return lax.ppermute(x, "rep", [(i, i ^ 1) for i in range(reps)])

    (sent,) = call(
        functools.partial(weigh_kernel, halves),
        [shape((owners, per_owner, 2 * bands, patches), BF16)],
        [VMEM] * 5 + [SMEM] * (1 + halves),
        [VMEM],
        [pltpu.VMEM((blocks, bands, patches), F32)],
    )(area, emission, reflect, total, other_core(total), row_ids, *col_ids)
    landed = lax.all_to_all(sent, "pairs", split_axis=0, concat_axis=0, tiled=True)
    extra = [geometry, *row_sides, *col_sides] if remade else []
    (total,) = call(
        functools.partial(second_kernel, bands, halves, remade),
        [total_shape],
        [VMEM, SMEM, VMEM] + [SMEM] * halves + [VMEM] * (halves + len(extra)),
        [VMEM],
        (),
        pair_flops,
    )(landed, row_ids, row_kept, *col_ids, *col_kept, *extra)
    return emission + reflect * (total + other_core(total))


def solution(mesh):
    placed = (
        P(None, "pairs", None),
        P(None, "pairs", None),
        P("pairs", None),
        P("pairs", None, None),
        P("pairs", None, None),
        P("pairs", "rep", None, None, None),
    )
    return jax.shard_map(
        shards, mesh=mesh, in_specs=placed, out_specs=P("pairs", None, None), check_vma=False
    )
```

```python
import functools
import math

import jax
import jax.numpy as jnp
from jax import lax
from jax.experimental import pallas as pl
from jax.experimental.pallas import tpu as pltpu
from jax.sharding import PartitionSpec as P

SOFTEN = 0.1
KEPT = 32
DEPTH = 48
F32 = jnp.float32
BF16 = jnp.bfloat16
VMEM = pl.BlockSpec(memory_space=pltpu.VMEM)
SMEM = pl.BlockSpec(memory_space=pltpu.SMEM)
HBM = pl.BlockSpec(memory_space=pltpu.HBM)


def loop(count, body):
    if count <= 16:
        for i in range(count):
            body(i)
    else:
        lax.fori_loop(0, count, lambda i, carry: (body(i), carry)[1], 0)


def owner_at(place, owners):
    if isinstance(place, int):
        return (place + owners // 2) % owners
    return lax.rem(place + owners // 2, owners)


def pieces(value, count):
    parts = []
    for _ in range(count):
        part = value.astype(BF16).astype(F32)
        parts.append(part)
        value = value - part
    return parts


def dot_rows(a, b):
    return a[0] * b[0] + a[1] * b[1] + a[2] * b[2]


def with_ids(record, ids):
    rows = lax.broadcasted_iota(jnp.int32, record.shape, 0)
    return jnp.where(rows == record.shape[0] - 1, ids, record)


def read_id(ids):
    return ids[:, :128][0, 0].astype(jnp.int32)


def stage_kernel(
    bands,
    held_in,
    positions_in,
    facing_in,
    area_in,
    emission_in,
    reflect_in,
    table,
    geometry,
    sent,
    area,
    emission,
    reflect,
    held,
    positions,
    facing,
    done,
):
    moves = [
        pltpu.make_async_copy(src, dst, done.at[i])
        for i, (src, dst) in enumerate(
            (
                (facing_in, facing),
                (positions_in, positions),
                (area_in, area),
                (emission_in, emission),
                (held_in, held),
                (reflect_in, reflect),
            )
        )
    ]
    for move in moves:
        move.start()
    blocks, patches = area.shape
    capacity, _, owners = held.shape
    moves[0].wait()
    azimuth, elevation = facing[0], facing[1]
    level = jnp.cos(elevation)
    normal = [jnp.cos(azimuth) * level, jnp.sin(azimuth) * level, jnp.sin(elevation)]
    moves[1].wait()
    place = [positions[axis] for axis in range(3)]
    for axis in range(3):
        geometry[:, axis, :] = place[axis]
        geometry[:, 3 + axis, :] = normal[axis]
        high, middle, low = pieces(place[axis], 3)
        table[:, bands + axis, :] = high
        table[:, bands + 8 + axis, :] = middle
        table[:, bands + (6, 7, 14)[axis], :] = low
        high, low = pieces(normal[axis], 2)
        table[:, bands + 3 + axis, :] = high
        table[:, bands + 11 + axis, :] = low
    table[:, bands + 15, :] = jnp.zeros_like(azimuth)
    geometry[:, 6, :] = dot_rows(place, normal)
    geometry[:, 7, :] = dot_rows(place, place)
    moves[4].wait()
    lanes = lax.broadcasted_iota(jnp.int32, (1, patches), 1)
    moves[2].wait()
    moves[3].wait()
    table[:, :bands, :] = (area[...][:, None, :] * emission[...]).astype(BF16).astype(F32)

    def one(place):
        owner = owner_at(place, owners)
        for slot in range(capacity):
            row, col = held[slot, 0, owner], held[slot, 1, owner]
            filled = row >= 0
            row = jnp.where(filled, lax.rem(row, blocks), -1)
            col = jnp.where(filled, lax.rem(col, blocks), -1)
            ids = jnp.where(lanes < patches // 2, col.astype(F32), row.astype(F32))
            sent[place, slot] = with_ids(table[jnp.maximum(row, 0)], ids).astype(BF16)

    loop(owners, one)
    moves[5].wait()


def serve_kernel(copies, table, landed, sent, mirror):
    capacity = sent.shape[1]

    def one(slot):
        record = landed[slot].astype(F32)
        mirror[slot] = record[-16:].astype(BF16)
        ids = record[-1:]
        row = ids[:, ids.shape[1] // 2 :]
        answer = table[jnp.maximum(read_id(ids), 0)]
        answer = with_ids(answer, jnp.concatenate([row, row], axis=1)).astype(BF16)
        for copy in range(copies):
            sent[slot // capacity * copies + copy, slot % capacity] = answer

    loop(landed.shape[0], one)


def own_factors(tile):
    row = [tile[k : k + 1, :] for k in range(8)]
    none = jnp.zeros_like(row[0])
    unit = jnp.ones_like(none)

    def stack(*rows):
        return jnp.concatenate(rows, axis=0)

    n = list(zip(*[pieces(row[3 + k] * (1.0 / math.pi), 3) for k in range(3)]))
    c = pieces(row[6] * (-1.0 / math.pi), 3)
    near = stack(
        *n[0], none, none, none, n[0][0], n[0][1],
        *n[0], none, none, none, n[0][2], none,
        *n[1], none, none, none, none, none,
        *n[1], none, none, none, none, none,
        *n[2], none, none, none, c[0], c[1],
        none, none, none, none, none, none, c[2], none,
    )
    p = list(zip(*[pieces(row[k], 3) for k in range(3)]))
    away = stack(
        none, none, none, *p[0], none, none,
        none, none, none, *p[0], none, none,
        none, none, none, *p[1], none, none,
        none, none, none, *p[1], none, none,
        none, none, none, *p[2], none, none,
        -unit, -unit, -unit, none, none, none, none, none,
    )
    m = [[-2.0 * v for v in part] for part in p]
    e = pieces(row[7] + SOFTEN, 3)
    spread = stack(
        *m[0], none, none, none, m[0][0], m[0][1],
        *m[0], none, none, none, m[0][2], none,
        *m[1], none, none, none, none, none,
        *m[1], none, none, none, none, none,
        *m[2], none, none, none, e[0], e[1],
        none, none, none, unit, unit, unit, e[2], none,
    )
    return jnp.concatenate([near, away, spread], axis=1).astype(BF16)


def other_sides(bands, wide, sides):
    slots = wide.shape[0]

    def row(index):
        return wide[:, bands + index, :]

    place = [row(k) + row(8 + k) + row((6, 7, 14)[k]) for k in range(3)]
    normal = [row(3 + k) + row(11 + k) for k in range(3)]
    constants = pieces(dot_rows(place, normal), 3) + pieces(dot_rows(place, place), 3)
    constants += [jnp.ones_like(place[0]), jnp.zeros_like(place[0])]
    rows = lax.broadcasted_iota(jnp.int32, (8, wide.shape[2]), 0)
    for k, value in enumerate(constants):
        wide[:, bands + 16 + k, :] = value

    def side(slot):
        first = wide[slot, bands : bands + 8, :]
        second = wide[slot, bands + 8 : bands + 16, :]
        last = wide[slot, bands + 16 : bands + 24, :]
        with_ones = jnp.where(rows < 6, first, 1.0)
        sides[slot] = jnp.concatenate(
            [first, second, first, second, with_ones, last], axis=0
        ).astype(BF16)

    loop(slots, side)


def form_factors(side, factors):
    patches = side.shape[1]
    parts = lax.dot_general(
        side, factors, (((0,), (0,)), ((), ())), preferred_element_type=F32
    )
    near = parts[:, :patches]
    away = parts[:, patches : 2 * patches]
    spread = parts[:, 2 * patches :]
    inverse = pltpu.reciprocal(spread, approx=True)
    inverse = inverse * (2.0 - spread * inverse)
    value = jnp.maximum(near, 0.0) * jnp.maximum(away, 0.0) * (inverse * inverse)
    return value.astype(BF16)


def build_matrices(bands, geometry, landed, order, ids, kept, sides, wide):
    def widen(slot):
        record = landed[order(slot)].astype(F32)
        wide[slot, bands + 16 - record.shape[0] : bands + 16, :] = record
        ids[slot] = read_id(record[-1:])

    loop(wide.shape[0], widen)
    other_sides(bands, wide, sides)

    def build(slot):
        return form_factors(sides[slot], own_factors(geometry[jnp.maximum(ids[slot], 0)]))

    def keep(slot):
        kept[slot] = build(slot)

    loop(kept.shape[0], keep)
    return build


def first_sweep(bands, geometry, landed, order, ids, total, kept, sides, wide):
    build = build_matrices(bands, geometry, landed, order, ids, kept, sides, wide)

    def add(slot, matrix):
        own_id = ids[slot]
        weights = wide[slot, :bands, :].astype(BF16)
        terms = jnp.dot(weights, matrix, preferred_element_type=F32)
        total[jnp.maximum(own_id, 0)] += jnp.where(own_id >= 0, terms, 0.0)

    def add_kept(slot):
        add(slot, kept[slot])

    def add_built(slot):
        add(slot, build(slot))

    held, slots = kept.shape[0], wide.shape[0]
    loop(held, add_kept)
    if held < slots:
        lax.fori_loop(held, slots, lambda i, carry: (add_built(i), carry)[1], 0)


def column_kernel(bands, geometry, landed, total, kept, ids, sides, wide):
    total[...] = jnp.zeros_like(total)
    first_sweep(bands, geometry, landed, lambda i: i, ids, total, kept, sides, wide)


def other_column_kernel(bands, geometry, landed, after, kept, ids, sides, wide):
    build_matrices(bands, geometry, landed, lambda i: i, ids, kept, sides, wide)


def row_kernel(bands, cores, halves, geometry, landed, before, total, kept, ids, sides, wide):
    capacity = landed.shape[0] // (lax.axis_size("pairs") * halves)
    here = lax.axis_index("rep") // cores

    def order(slot):
        owner, back, entry = slot // (halves * capacity), slot // capacity % halves, slot % capacity
        half = lax.rem(here + (halves - back), halves)
        return (owner * halves + half) * capacity + entry

    total[...] = before[...]
    first_sweep(bands, geometry, landed, order, ids, total, kept, sides, wide)


def add_kernel(parts, *refs):
    total = refs[0][...]
    for part in refs[1:parts]:
        total = total + part[...]
    refs[-1][...] = total


def weigh_kernel(halves, area, emission, reflect, mine, theirs, row_ids, *refs):
    col_ids = refs[:halves]
    sent, table = refs[halves:]
    radiosity = emission[...] + reflect[...] * (mine[...] + theirs[...])
    table[...] = area[...][:, None, :] * radiosity
    owners, twos = sent.shape[0], sent.shape[1]
    capacity = twos // halves

    def pick(owner, entry):
        if entry < twos:
            chosen = col_ids[entry // capacity][owner * capacity + entry % capacity]
        else:
            chosen = row_ids[owner * twos + entry - twos]
        return table[jnp.maximum(chosen, 0)]

    def one(owner):
        for two in range(twos):
            both = jnp.concatenate([pick(owner, 2 * two), pick(owner, 2 * two + 1)], axis=0)
            sent[owner, two] = both.astype(BF16)

    loop(owners, one)


def second_kernel(bands, halves, remade, landed, row_ids, row_kept, *refs):
    col_ids, col_kept = refs[:halves], refs[halves : 2 * halves]
    total = refs[-1]
    if remade:
        geometry, row_sides, *col_sides = refs[2 * halves : -1]
    total[...] = jnp.zeros_like(total)
    owners, twos = landed.shape[0], landed.shape[1]
    capacity = twos // halves

    def one(owner):
        for entry in range(2 * twos):
            part = entry // capacity - halves
            if entry < twos:
                ids, kept, slot = row_ids, row_kept, owner * twos + entry
            else:
                ids, kept = col_ids[part], col_kept[part]
                slot = owner * capacity + entry % capacity
            own_id = ids[slot]
            own = jnp.maximum(own_id, 0)
            weights = landed[owner, entry // 2]
            half = (entry % 2) * bands

            def add(matrix, own_id=own_id, own=own, weights=weights, half=half):
                terms = jnp.dot(weights, matrix, preferred_element_type=F32)
                total[own] += jnp.where(own_id >= 0, terms[half : half + bands], 0.0)

            if not remade:
                add(kept[slot])
                continue
            sides = row_sides if entry < twos else col_sides[part]

            def from_kept(slot=slot, kept=kept, add=add):
                add(kept[slot])

            def from_sides(slot=slot, own=own, sides=sides, add=add):
                add(form_factors(sides[slot], own_factors(geometry[own])))

            held = kept.shape[0]
            pl.when((own_id >= 0) & (slot < held))(from_kept)
            pl.when((own_id >= 0) & (slot >= held))(from_sides)

    loop(owners, one)


def in_hbm(x):
    return pltpu.with_memory_space_constraint(x, pltpu.HBM)


def in_smem(x):
    return pltpu.with_memory_space_constraint(x, pltpu.SMEM)


def call(kernel, outs, ins, out_specs, scratch=(), flops=0):
    sizes = [math.prod(s.shape) * s.dtype.itemsize for s in outs]
    held = [math.prod(s.shape) * s.dtype.itemsize for s in scratch if s.dtype in (F32, BF16)]
    room = 2 * sum(sizes) + sum(held) + 8 * 1024 * 1024
    return pl.pallas_call(
        kernel,
        out_shape=[
            spec.memory_space(s.shape, s.dtype) for s, spec in zip(outs, out_specs)
        ],
        in_specs=ins,
        out_specs=out_specs,
        scratch_shapes=scratch,
        compiler_params=pltpu.CompilerParams(vmem_limit_bytes=room),
        cost_estimate=pl.CostEstimate(flops=flops, bytes_accessed=sum(sizes), transcendentals=0),
    )


def shards(positions, facing, area, emission, reflect, pair_list):
    blocks, bands, patches = emission.shape
    owners = lax.axis_size("pairs")
    reps = lax.axis_size("rep")
    cores = 2 if reps % 2 == 0 else 1
    halves = reps // cores
    held = jnp.transpose(pair_list[0, 0], (1, 2, 0))
    capacity = held.shape[0]
    per_owner = halves * capacity
    slots = owners * per_owner
    near_slots = owners * capacity
    remade = slots > KEPT
    rows = bands + 16
    shape = jax.ShapeDtypeStruct
    total_shape = shape((blocks, bands, patches), F32)
    pair_flops = slots * patches * patches * 50

    def kept_of(count):
        return shape((min(count, KEPT), patches, patches), BF16)

    def sweep_room(count):
        sides = shape((count, DEPTH, patches), BF16)
        wide = pltpu.VMEM((count, rows + 8, patches), F32)
        if remade:
            return [sides], [wide]
        return [], [pltpu.VMEM(sides.shape, BF16), wide]

    table, geometry, sent, area, emission, reflect = call(
        functools.partial(stage_kernel, bands),
        [
            shape((blocks, rows, patches), F32),
            shape((blocks, 8, patches), F32),
            shape((owners, capacity, rows, patches), BF16),
            shape(area.shape, F32),
            total_shape,
            total_shape,
        ],
        [HBM] * 6,
        [VMEM] * 6,
        [
            pltpu.SMEM(held.shape, jnp.int32),
            pltpu.VMEM(positions.shape, F32),
            pltpu.VMEM(facing.shape, F32),
            pltpu.SemaphoreType.DMA((6,)),
        ],
    )(*[in_hbm(x) for x in (held, positions, facing, area, emission, reflect)])
    owner_order = [owner_at(place, owners) for place in range(owners)]

    def exchange(x):
        return lax.all_to_all(
            x,
            "pairs",
            split_axis=0,
            concat_axis=0,
            tiled=True,
            axis_index_groups=[owner_order],
        )

    landed = exchange(sent)
    col_side = landed.reshape(near_slots, rows, patches)
    sent, mirror = call(
        functools.partial(serve_kernel, halves),
        [
            shape((owners * halves, capacity, rows, patches), BF16),
            shape((near_slots, 16, patches), BF16),
        ],
        [VMEM, VMEM],
        [VMEM, VMEM],
    )(table, col_side)
    same_core = [
        [owner * reps + half * cores + core for owner in owner_order for half in range(halves)]
        for core in range(cores)
    ]
    landed = lax.all_to_all(
        sent,
        ("pairs", "rep"),
        split_axis=0,
        concat_axis=0,
        tiled=True,
        axis_index_groups=same_core,
    )
    row_side = landed.reshape(slots, rows, patches)

    def other_halves(x):
        return [
            lax.ppermute(x, "rep", [(i, (i + back * cores) % reps) for i in range(reps)])
            for back in range(1, halves)
        ]

    mirrors = other_halves(mirror)
    near_ids = shape((near_slots,), jnp.int32)
    outs, room = sweep_room(near_slots)
    col_total, kept, ids, *sides = call(
        functools.partial(column_kernel, bands),
        [total_shape, kept_of(near_slots), near_ids] + outs,
        [VMEM, VMEM],
        [VMEM, VMEM, SMEM] + [VMEM] * len(outs),
        room,
        pair_flops // halves,
    )(geometry, col_side)
    col_ids, col_kept, col_sides = [in_smem(ids)], [kept], [*sides]
    far_totals = other_halves(col_total)
    outs, room = sweep_room(slots)
    total, row_kept, row_ids, *row_sides = call(
        functools.partial(row_kernel, bands, cores, halves),
        [total_shape, kept_of(slots), shape((slots,), jnp.int32)] + outs,
        [VMEM, VMEM, VMEM],
        [VMEM, VMEM, SMEM] + [VMEM] * len(outs),
        room,
        pair_flops,
    )(geometry, row_side, col_total)
    row_ids = in_smem(row_ids)
    if far_totals:
        (total,) = call(
            functools.partial(add_kernel, halves),
            [total_shape],
            [VMEM] * (halves + len(mirrors)),
            [VMEM],
        )(total, *far_totals, *mirrors)
    outs, room = sweep_room(near_slots)
    for mirror in mirrors:
        kept, ids, *sides = call(
            functools.partial(other_column_kernel, bands),
            [kept_of(near_slots), near_ids] + outs,
            [VMEM, VMEM, VMEM],
            [VMEM, SMEM] + [VMEM] * len(outs),
            room,
            pair_flops // halves,
        )(geometry, mirror, total)
        col_ids.append(in_smem(ids))
        col_kept.append(kept)
        col_sides.extend(sides)

    def other_core(x):
        if cores == 1:
            return jnp.zeros_like(x)
        return lax.ppermute(x, "rep", [(i, i ^ 1) for i in range(reps)])

    (sent,) = call(
        functools.partial(weigh_kernel, halves),
        [shape((owners, per_owner, 2 * bands, patches), BF16)],
        [VMEM] * 5 + [SMEM] * (1 + halves),
        [VMEM],
        [pltpu.VMEM((blocks, bands, patches), F32)],
    )(area, emission, reflect, total, other_core(total), row_ids, *col_ids)
    landed = exchange(sent)
    extra = [geometry, *row_sides, *col_sides] if remade else []
    (total,) = call(
        functools.partial(second_kernel, bands, halves, remade),
        [total_shape],
        [VMEM, SMEM, VMEM] + [SMEM] * halves + [VMEM] * (halves + len(extra)),
        [VMEM],
        (),
        pair_flops,
    )(landed, row_ids, row_kept, *col_ids, *col_kept, *extra)
    return emission + reflect * (total + other_core(total))


def solution(mesh):
    placed = (
        P(None, "pairs", None),
        P(None, "pairs", None),
        P("pairs", None),
        P("pairs", None, None),
        P("pairs", None, None),
        P("pairs", "rep", None, None, None),
    )
    return jax.shard_map(
        shards, mesh=mesh, in_specs=placed, out_specs=P("pairs", None, None), check_vma=False
    )
```

```python
import functools
import math

import jax
import jax.numpy as jnp
from jax import lax
from jax.experimental import pallas as pl
from jax.experimental.pallas import tpu as pltpu
from jax.sharding import PartitionSpec as P

SOFTEN = 0.1
KEPT = 32
DEPTH = 48
F32 = jnp.float32
BF16 = jnp.bfloat16
VMEM = pl.BlockSpec(memory_space=pltpu.VMEM)
SMEM = pl.BlockSpec(memory_space=pltpu.SMEM)
HBM = pl.BlockSpec(memory_space=pltpu.HBM)


def loop(count, body):
    if count <= 16:
        for i in range(count):
            body(i)
    else:
        lax.fori_loop(0, count, lambda i, carry: (body(i), carry)[1], 0)


def owner_at(place, owners):
    if isinstance(place, int):
        return (place + owners // 2 + 1) % owners
    return lax.rem(place + owners // 2 + 1, owners)


def pieces(value, count):
    parts = []
    for _ in range(count):
        part = value.astype(BF16).astype(F32)
        parts.append(part)
        value = value - part
    return parts


def dot_rows(a, b):
    return a[0] * b[0] + a[1] * b[1] + a[2] * b[2]


def with_ids(record, ids):
    rows = lax.broadcasted_iota(jnp.int32, record.shape, 0)
    return jnp.where(rows == record.shape[0] - 1, ids, record)


def read_id(ids):
    return ids[:, :128][0, 0].astype(jnp.int32)


def stage_kernel(
    bands,
    held_in,
    positions_in,
    facing_in,
    area_in,
    emission_in,
    reflect_in,
    table,
    geometry,
    sent,
    area,
    emission,
    reflect,
    held,
    positions,
    facing,
    done,
):
    moves = [
        pltpu.make_async_copy(src, dst, done.at[i])
        for i, (src, dst) in enumerate(
            (
                (facing_in, facing),
                (positions_in, positions),
                (area_in, area),
                (emission_in, emission),
                (held_in, held),
                (reflect_in, reflect),
            )
        )
    ]
    for move in moves:
        move.start()
    blocks, patches = area.shape
    capacity, _, owners = held.shape
    moves[0].wait()
    azimuth, elevation = facing[0], facing[1]
    level = jnp.cos(elevation)
    normal = [jnp.cos(azimuth) * level, jnp.sin(azimuth) * level, jnp.sin(elevation)]
    moves[1].wait()
    place = [positions[axis] for axis in range(3)]
    for axis in range(3):
        geometry[:, axis, :] = place[axis]
        geometry[:, 3 + axis, :] = normal[axis]
        high, middle, low = pieces(place[axis], 3)
        table[:, bands + axis, :] = high
        table[:, bands + 8 + axis, :] = middle
        table[:, bands + (6, 7, 14)[axis], :] = low
        high, low = pieces(normal[axis], 2)
        table[:, bands + 3 + axis, :] = high
        table[:, bands + 11 + axis, :] = low
    table[:, bands + 15, :] = jnp.zeros_like(azimuth)
    geometry[:, 6, :] = dot_rows(place, normal)
    geometry[:, 7, :] = dot_rows(place, place)
    moves[4].wait()
    lanes = lax.broadcasted_iota(jnp.int32, (1, patches), 1)
    moves[2].wait()
    moves[3].wait()
    table[:, :bands, :] = (area[...][:, None, :] * emission[...]).astype(BF16).astype(F32)

    def one(place):
        owner = owner_at(place, owners)
        for slot in range(capacity):
            row, col = held[slot, 0, owner], held[slot, 1, owner]
            filled = row >= 0
            row = jnp.where(filled, lax.rem(row, blocks), -1)
            col = jnp.where(filled, lax.rem(col, blocks), -1)
            ids = jnp.where(lanes < patches // 2, col.astype(F32), row.astype(F32))
            sent[place, slot] = with_ids(table[jnp.maximum(row, 0)], ids).astype(BF16)

    loop(owners, one)
    moves[5].wait()


def serve_kernel(copies, table, landed, sent, mirror):
    capacity = sent.shape[1]

    def one(slot):
        record = landed[slot].astype(F32)
        mirror[slot] = record[-16:].astype(BF16)
        ids = record[-1:]
        row = ids[:, ids.shape[1] // 2 :]
        answer = table[jnp.maximum(read_id(ids), 0)]
        answer = with_ids(answer, jnp.concatenate([row, row], axis=1)).astype(BF16)
        for copy in range(copies):
            sent[slot // capacity * copies + copy, slot % capacity] = answer

    loop(landed.shape[0], one)


def own_factors(tile):
    row = [tile[k : k + 1, :] for k in range(8)]
    none = jnp.zeros_like(row[0])
    unit = jnp.ones_like(none)

    def stack(*rows):
        return jnp.concatenate(rows, axis=0)

    n = list(zip(*[pieces(row[3 + k] * (1.0 / math.pi), 3) for k in range(3)]))
    c = pieces(row[6] * (-1.0 / math.pi), 3)
    near = stack(
        *n[0], none, none, none, n[0][0], n[0][1],
        *n[0], none, none, none, n[0][2], none,
        *n[1], none, none, none, none, none,
        *n[1], none, none, none, none, none,
        *n[2], none, none, none, c[0], c[1],
        none, none, none, none, none, none, c[2], none,
    )
    p = list(zip(*[pieces(row[k], 3) for k in range(3)]))
    away = stack(
        none, none, none, *p[0], none, none,
        none, none, none, *p[0], none, none,
        none, none, none, *p[1], none, none,
        none, none, none, *p[1], none, none,
        none, none, none, *p[2], none, none,
        -unit, -unit, -unit, none, none, none, none, none,
    )
    m = [[-2.0 * v for v in part] for part in p]
    e = pieces(row[7] + SOFTEN, 3)
    spread = stack(
        *m[0], none, none, none, m[0][0], m[0][1],
        *m[0], none, none, none, m[0][2], none,
        *m[1], none, none, none, none, none,
        *m[1], none, none, none, none, none,
        *m[2], none, none, none, e[0], e[1],
        none, none, none, unit, unit, unit, e[2], none,
    )
    return jnp.concatenate([near, away, spread], axis=1).astype(BF16)


def other_sides(bands, wide, sides):
    slots = wide.shape[0]

    def row(index):
        return wide[:, bands + index, :]

    place = [row(k) + row(8 + k) + row((6, 7, 14)[k]) for k in range(3)]
    normal = [row(3 + k) + row(11 + k) for k in range(3)]
    constants = pieces(dot_rows(place, normal), 3) + pieces(dot_rows(place, place), 3)
    constants += [jnp.ones_like(place[0]), jnp.zeros_like(place[0])]
    rows = lax.broadcasted_iota(jnp.int32, (8, wide.shape[2]), 0)
    for k, value in enumerate(constants):
        wide[:, bands + 16 + k, :] = value

    def side(slot):
        first = wide[slot, bands : bands + 8, :]
        second = wide[slot, bands + 8 : bands + 16, :]
        last = wide[slot, bands + 16 : bands + 24, :]
        with_ones = jnp.where(rows < 6, first, 1.0)
        sides[slot] = jnp.concatenate(
            [first, second, first, second, with_ones, last], axis=0
        ).astype(BF16)

    loop(slots, side)


def form_factors(side, factors):
    patches = side.shape[1]
    parts = lax.dot_general(
        side, factors, (((0,), (0,)), ((), ())), preferred_element_type=F32
    )
    near = parts[:, :patches]
    away = parts[:, patches : 2 * patches]
    spread = parts[:, 2 * patches :]
    inverse = pltpu.reciprocal(spread, approx=True)
    inverse = inverse * (2.0 - spread * inverse)
    value = jnp.maximum(near, 0.0) * jnp.maximum(away, 0.0) * (inverse * inverse)
    return value.astype(BF16)


def build_matrices(bands, geometry, landed, order, ids, kept, sides, wide):
    def widen(slot):
        record = landed[order(slot)].astype(F32)
        wide[slot, bands + 16 - record.shape[0] : bands + 16, :] = record
        ids[slot] = read_id(record[-1:])

    loop(wide.shape[0], widen)
    other_sides(bands, wide, sides)

    def build(slot):
        return form_factors(sides[slot], own_factors(geometry[jnp.maximum(ids[slot], 0)]))

    def keep(slot):
        kept[slot] = build(slot)

    loop(kept.shape[0], keep)
    return build


def first_sweep(bands, geometry, landed, order, ids, total, kept, sides, wide):
    build = build_matrices(bands, geometry, landed, order, ids, kept, sides, wide)

    def add(slot, matrix):
        own_id = ids[slot]
        weights = wide[slot, :bands, :].astype(BF16)
        terms = jnp.dot(weights, matrix, preferred_element_type=F32)
        total[jnp.maximum(own_id, 0)] += jnp.where(own_id >= 0, terms, 0.0)

    def add_kept(slot):
        add(slot, kept[slot])

    def add_built(slot):
        add(slot, build(slot))

    held, slots = kept.shape[0], wide.shape[0]
    loop(held, add_kept)
    if held < slots:
        lax.fori_loop(held, slots, lambda i, carry: (add_built(i), carry)[1], 0)


def column_kernel(bands, geometry, landed, total, kept, ids, sides, wide):
    total[...] = jnp.zeros_like(total)
    first_sweep(bands, geometry, landed, lambda i: i, ids, total, kept, sides, wide)


def other_column_kernel(bands, geometry, landed, after, kept, ids, sides, wide):
    build_matrices(bands, geometry, landed, lambda i: i, ids, kept, sides, wide)


def row_kernel(bands, cores, halves, geometry, landed, before, total, kept, ids, sides, wide):
    capacity = landed.shape[0] // (lax.axis_size("pairs") * halves)
    here = lax.axis_index("rep") // cores

    def order(slot):
        owner, back, entry = slot // (halves * capacity), slot // capacity % halves, slot % capacity
        half = lax.rem(here + (halves - back), halves)
        return (owner * halves + (halves - 1 - half)) * capacity + entry

    total[...] = before[...]
    first_sweep(bands, geometry, landed, order, ids, total, kept, sides, wide)


def add_kernel(parts, *refs):
    total = refs[0][...]
    for part in refs[1:parts]:
        total = total + part[...]
    refs[-1][...] = total


def weigh_kernel(halves, area, emission, reflect, mine, theirs, row_ids, *refs):
    col_ids = refs[:halves]
    sent, table = refs[halves:]
    radiosity = emission[...] + reflect[...] * (mine[...] + theirs[...])
    table[...] = area[...][:, None, :] * radiosity
    owners, twos = sent.shape[0], sent.shape[1]
    capacity = twos // halves

    def pick(owner, entry):
        if entry < twos:
            chosen = col_ids[entry // capacity][owner * capacity + entry % capacity]
        else:
            chosen = row_ids[owner * twos + entry - twos]
        return table[jnp.maximum(chosen, 0)]

    def one(owner):
        for two in range(twos):
            both = jnp.concatenate([pick(owner, 2 * two), pick(owner, 2 * two + 1)], axis=0)
            sent[owner, two] = both.astype(BF16)

    loop(owners, one)


def second_kernel(bands, halves, remade, landed, row_ids, row_kept, *refs):
    col_ids, col_kept = refs[:halves], refs[halves : 2 * halves]
    total = refs[-1]
    if remade:
        geometry, row_sides, *col_sides = refs[2 * halves : -1]
    total[...] = jnp.zeros_like(total)
    owners, twos = landed.shape[0], landed.shape[1]
    capacity = twos // halves

    def one(owner):
        for entry in range(2 * twos):
            part = entry // capacity - halves
            if entry < twos:
                ids, kept, slot = row_ids, row_kept, owner * twos + entry
            else:
                ids, kept = col_ids[part], col_kept[part]
                slot = owner * capacity + entry % capacity
            own_id = ids[slot]
            own = jnp.maximum(own_id, 0)
            weights = landed[owner, entry // 2]
            half = (entry % 2) * bands

            def add(matrix, own_id=own_id, own=own, weights=weights, half=half):
                terms = jnp.dot(weights, matrix, preferred_element_type=F32)
                total[own] += jnp.where(own_id >= 0, terms[half : half + bands], 0.0)

            if not remade:
                add(kept[slot])
                continue
            sides = row_sides if entry < twos else col_sides[part]

            def from_kept(slot=slot, kept=kept, add=add):
                add(kept[slot])

            def from_sides(slot=slot, own=own, sides=sides, add=add):
                add(form_factors(sides[slot], own_factors(geometry[own])))

            held = kept.shape[0]
            pl.when((own_id >= 0) & (slot < held))(from_kept)
            pl.when((own_id >= 0) & (slot >= held))(from_sides)

    loop(owners, one)


def in_hbm(x):
    return pltpu.with_memory_space_constraint(x, pltpu.HBM)


def in_smem(x):
    return pltpu.with_memory_space_constraint(x, pltpu.SMEM)


def call(kernel, outs, ins, out_specs, scratch=(), flops=0):
    sizes = [math.prod(s.shape) * s.dtype.itemsize for s in outs]
    held = [math.prod(s.shape) * s.dtype.itemsize for s in scratch if s.dtype in (F32, BF16)]
    room = 2 * sum(sizes) + sum(held) + 8 * 1024 * 1024
    return pl.pallas_call(
        kernel,
        out_shape=[
            spec.memory_space(s.shape, s.dtype) for s, spec in zip(outs, out_specs)
        ],
        in_specs=ins,
        out_specs=out_specs,
        scratch_shapes=scratch,
        compiler_params=pltpu.CompilerParams(vmem_limit_bytes=room),
        cost_estimate=pl.CostEstimate(flops=flops, bytes_accessed=sum(sizes), transcendentals=0),
    )


def shards(positions, facing, area, emission, reflect, pair_list):
    blocks, bands, patches = emission.shape
    owners = lax.axis_size("pairs")
    reps = lax.axis_size("rep")
    cores = 2 if reps % 2 == 0 else 1
    halves = reps // cores
    held = jnp.transpose(pair_list[0, 0], (1, 2, 0))
    capacity = held.shape[0]
    per_owner = halves * capacity
    slots = owners * per_owner
    near_slots = owners * capacity
    remade = slots > KEPT
    rows = bands + 16
    shape = jax.ShapeDtypeStruct
    total_shape = shape((blocks, bands, patches), F32)
    pair_flops = slots * patches * patches * 50

    def kept_of(count):
        return shape((min(count, KEPT), patches, patches), BF16)

    def sweep_room(count):
        sides = shape((count, DEPTH, patches), BF16)
        wide = pltpu.VMEM((count, rows + 8, patches), F32)
        if remade:
            return [sides], [wide]
        return [], [pltpu.VMEM(sides.shape, BF16), wide]

    table, geometry, sent, area, emission, reflect = call(
        functools.partial(stage_kernel, bands),
        [
            shape((blocks, rows, patches), F32),
            shape((blocks, 8, patches), F32),
            shape((owners, capacity, rows, patches), BF16),
            shape(area.shape, F32),
            total_shape,
            total_shape,
        ],
        [HBM] * 6,
        [VMEM] * 6,
        [
            pltpu.SMEM(held.shape, jnp.int32),
            pltpu.VMEM(positions.shape, F32),
            pltpu.VMEM(facing.shape, F32),
            pltpu.SemaphoreType.DMA((6,)),
        ],
    )(*[in_hbm(x) for x in (held, positions, facing, area, emission, reflect)])
    owner_order = [owner_at(place, owners) for place in range(owners)]

    def exchange(x):
        return lax.all_to_all(
            x,
            "pairs",
            split_axis=0,
            concat_axis=0,
            tiled=True,
            axis_index_groups=[owner_order],
        )

    landed = exchange(sent)
    col_side = landed.reshape(near_slots, rows, patches)
    sent, mirror = call(
        functools.partial(serve_kernel, halves),
        [
            shape((owners * halves, capacity, rows, patches), BF16),
            shape((near_slots, 16, patches), BF16),
        ],
        [VMEM, VMEM],
        [VMEM, VMEM],
    )(table, col_side)
    same_core = [
        [owner * reps + half * cores + core for owner in owner_order for half in reversed(range(halves))]
        for core in range(cores)
    ]
    landed = lax.all_to_all(
        sent,
        ("pairs", "rep"),
        split_axis=0,
        concat_axis=0,
        tiled=True,
        axis_index_groups=same_core,
    )
    row_side = landed.reshape(slots, rows, patches)

    def other_halves(x):
        return [
            lax.ppermute(x, "rep", [(i, (i + back * cores) % reps) for i in range(reps)])
            for back in range(1, halves)
        ]

    mirrors = other_halves(mirror)
    near_ids = shape((near_slots,), jnp.int32)
    outs, room = sweep_room(near_slots)
    col_total, kept, ids, *sides = call(
        functools.partial(column_kernel, bands),
        [total_shape, kept_of(near_slots), near_ids] + outs,
        [VMEM, VMEM],
        [VMEM, VMEM, SMEM] + [VMEM] * len(outs),
        room,
        pair_flops // halves,
    )(geometry, col_side)
    col_ids, col_kept, col_sides = [in_smem(ids)], [kept], [*sides]
    far_totals = other_halves(col_total)
    outs, room = sweep_room(slots)
    total, row_kept, row_ids, *row_sides = call(
        functools.partial(row_kernel, bands, cores, halves),
        [total_shape, kept_of(slots), shape((slots,), jnp.int32)] + outs,
        [VMEM, VMEM, VMEM],
        [VMEM, VMEM, SMEM] + [VMEM] * len(outs),
        room,
        pair_flops,
    )(geometry, row_side, col_total)
    row_ids = in_smem(row_ids)
    if far_totals:
        (total,) = call(
            functools.partial(add_kernel, halves),
            [total_shape],
            [VMEM] * (halves + len(mirrors)),
            [VMEM],
        )(total, *far_totals, *mirrors)
    outs, room = sweep_room(near_slots)
    for mirror in mirrors:
        kept, ids, *sides = call(
            functools.partial(other_column_kernel, bands),
            [kept_of(near_slots), near_ids] + outs,
            [VMEM, VMEM, VMEM],
            [VMEM, SMEM] + [VMEM] * len(outs),
            room,
            pair_flops // halves,
        )(geometry, mirror, total)
        col_ids.append(in_smem(ids))
        col_kept.append(kept)
        col_sides.extend(sides)

    def other_core(x):
        if cores == 1:
            return jnp.zeros_like(x)
        return lax.ppermute(x, "rep", [(i, i ^ 1) for i in range(reps)])

    (sent,) = call(
        functools.partial(weigh_kernel, halves),
        [shape((owners, per_owner, 2 * bands, patches), BF16)],
        [VMEM] * 5 + [SMEM] * (1 + halves),
        [VMEM],
        [pltpu.VMEM((blocks, bands, patches), F32)],
    )(area, emission, reflect, total, other_core(total), row_ids, *col_ids)
    landed = exchange(sent)
    extra = [geometry, *row_sides, *col_sides] if remade else []
    (total,) = call(
        functools.partial(second_kernel, bands, halves, remade),
        [total_shape],
        [VMEM, SMEM, VMEM] + [SMEM] * halves + [VMEM] * (halves + len(extra)),
        [VMEM],
        (),
        pair_flops,
    )(landed, row_ids, row_kept, *col_ids, *col_kept, *extra)
    return emission + reflect * (total + other_core(total))


def solution(mesh):
    placed = (
        P(None, "pairs", None),
        P(None, "pairs", None),
        P("pairs", None),
        P("pairs", None, None),
        P("pairs", None, None),
        P("pairs", "rep", None, None, None),
    )
    return jax.shard_map(
        shards, mesh=mesh, in_specs=placed, out_specs=P("pairs", None, None), check_vma=False
    )
```

```python
import functools
import math

import jax
import jax.numpy as jnp
from jax import lax
from jax.experimental import pallas as pl
from jax.experimental.pallas import tpu as pltpu
from jax.sharding import PartitionSpec as P

SOFTEN = 0.1
KEPT = 32
DEPTH = 48
F32 = jnp.float32
BF16 = jnp.bfloat16
VMEM = pl.BlockSpec(memory_space=pltpu.VMEM)
SMEM = pl.BlockSpec(memory_space=pltpu.SMEM)
HBM = pl.BlockSpec(memory_space=pltpu.HBM)


def loop(count, body):
    if count <= 16:
        for i in range(count):
            body(i)
    else:
        lax.fori_loop(0, count, lambda i, carry: (body(i), carry)[1], 0)


def owner_at(place, owners):
    first = owners // 2 + 1
    if owners & (owners - 1) == 0 and owners > 2:
        return place ^ first
    if isinstance(place, int):
        return (place + first) % owners
    return lax.rem(place + first, owners)


def pieces(value, count):
    parts = []
    for _ in range(count):
        part = value.astype(BF16).astype(F32)
        parts.append(part)
        value = value - part
    return parts


def dot_rows(a, b):
    return a[0] * b[0] + a[1] * b[1] + a[2] * b[2]


def with_ids(record, ids):
    rows = lax.broadcasted_iota(jnp.int32, record.shape, 0)
    return jnp.where(rows == record.shape[0] - 1, ids, record)


def read_id(ids):
    return ids[:, :128][0, 0].astype(jnp.int32)


def stage_kernel(
    bands,
    held_in,
    positions_in,
    facing_in,
    area_in,
    emission_in,
    reflect_in,
    table,
    geometry,
    sent,
    area,
    emission,
    reflect,
    held,
    positions,
    facing,
    done,
):
    moves = [
        pltpu.make_async_copy(src, dst, done.at[i])
        for i, (src, dst) in enumerate(
            (
                (facing_in, facing),
                (positions_in, positions),
                (area_in, area),
                (emission_in, emission),
                (held_in, held),
                (reflect_in, reflect),
            )
        )
    ]
    for move in moves:
        move.start()
    blocks, patches = area.shape
    capacity, _, owners = held.shape
    moves[0].wait()
    azimuth, elevation = facing[0], facing[1]
    level = jnp.cos(elevation)
    normal = [jnp.cos(azimuth) * level, jnp.sin(azimuth) * level, jnp.sin(elevation)]
    moves[1].wait()
    place = [positions[axis] for axis in range(3)]
    for axis in range(3):
        geometry[:, axis, :] = place[axis]
        geometry[:, 3 + axis, :] = normal[axis]
        high, middle, low = pieces(place[axis], 3)
        table[:, bands + axis, :] = high
        table[:, bands + 8 + axis, :] = middle
        table[:, bands + (6, 7, 14)[axis], :] = low
        high, low = pieces(normal[axis], 2)
        table[:, bands + 3 + axis, :] = high
        table[:, bands + 11 + axis, :] = low
    table[:, bands + 15, :] = jnp.zeros_like(azimuth)
    geometry[:, 6, :] = dot_rows(place, normal)
    geometry[:, 7, :] = dot_rows(place, place)
    moves[4].wait()
    lanes = lax.broadcasted_iota(jnp.int32, (1, patches), 1)
    moves[2].wait()
    moves[3].wait()
    table[:, :bands, :] = (area[...][:, None, :] * emission[...]).astype(BF16).astype(F32)

    def one(place):
        owner = owner_at(place, owners)
        for slot in range(capacity):
            row, col = held[slot, 0, owner], held[slot, 1, owner]
            filled = row >= 0
            row = jnp.where(filled, lax.rem(row, blocks), -1)
            col = jnp.where(filled, lax.rem(col, blocks), -1)
            ids = jnp.where(lanes < patches // 2, col.astype(F32), row.astype(F32))
            sent[place, slot] = with_ids(table[jnp.maximum(row, 0)], ids).astype(BF16)

    loop(owners, one)
    moves[5].wait()


def serve_kernel(copies, table, landed, sent, mirror):
    capacity = sent.shape[1]

    def one(slot):
        record = landed[slot].astype(F32)
        mirror[slot] = record[-16:].astype(BF16)
        ids = record[-1:]
        row = ids[:, ids.shape[1] // 2 :]
        answer = table[jnp.maximum(read_id(ids), 0)]
        answer = with_ids(answer, jnp.concatenate([row, row], axis=1)).astype(BF16)
        for copy in range(copies):
            sent[slot // capacity * copies + copy, slot % capacity] = answer

    loop(landed.shape[0], one)


def own_factors(tile):
    row = [tile[k : k + 1, :] for k in range(8)]
    none = jnp.zeros_like(row[0])
    unit = jnp.ones_like(none)

    def stack(*rows):
        return jnp.concatenate(rows, axis=0)

    n = list(zip(*[pieces(row[3 + k] * (1.0 / math.pi), 3) for k in range(3)]))
    c = pieces(row[6] * (-1.0 / math.pi), 3)
    near = stack(
        *n[0], none, none, none, n[0][0], n[0][1],
        *n[0], none, none, none, n[0][2], none,
        *n[1], none, none, none, none, none,
        *n[1], none, none, none, none, none,
        *n[2], none, none, none, c[0], c[1],
        none, none, none, none, none, none, c[2], none,
    )
    p = list(zip(*[pieces(row[k], 3) for k in range(3)]))
    away = stack(
        none, none, none, *p[0], none, none,
        none, none, none, *p[0], none, none,
        none, none, none, *p[1], none, none,
        none, none, none, *p[1], none, none,
        none, none, none, *p[2], none, none,
        -unit, -unit, -unit, none, none, none, none, none,
    )
    m = [[-2.0 * v for v in part] for part in p]
    e = pieces(row[7] + SOFTEN, 3)
    spread = stack(
        *m[0], none, none, none, m[0][0], m[0][1],
        *m[0], none, none, none, m[0][2], none,
        *m[1], none, none, none, none, none,
        *m[1], none, none, none, none, none,
        *m[2], none, none, none, e[0], e[1],
        none, none, none, unit, unit, unit, e[2], none,
    )
    return jnp.concatenate([near, away, spread], axis=1).astype(BF16)


def other_sides(bands, wide, sides):
    slots = wide.shape[0]

    def row(index):
        return wide[:, bands + index, :]

    place = [row(k) + row(8 + k) + row((6, 7, 14)[k]) for k in range(3)]
    normal = [row(3 + k) + row(11 + k) for k in range(3)]
    constants = pieces(dot_rows(place, normal), 3) + pieces(dot_rows(place, place), 3)
    constants += [jnp.ones_like(place[0]), jnp.zeros_like(place[0])]
    rows = lax.broadcasted_iota(jnp.int32, (8, wide.shape[2]), 0)
    for k, value in enumerate(constants):
        wide[:, bands + 16 + k, :] = value

    def side(slot):
        first = wide[slot, bands : bands + 8, :]
        second = wide[slot, bands + 8 : bands + 16, :]
        last = wide[slot, bands + 16 : bands + 24, :]
        with_ones = jnp.where(rows < 6, first, 1.0)
        sides[slot] = jnp.concatenate(
            [first, second, first, second, with_ones, last], axis=0
        ).astype(BF16)

    loop(slots, side)


def form_factors(side, factors):
    patches = side.shape[1]
    parts = lax.dot_general(
        side, factors, (((0,), (0,)), ((), ())), preferred_element_type=F32
    )
    near = parts[:, :patches]
    away = parts[:, patches : 2 * patches]
    spread = parts[:, 2 * patches :]
    inverse = pltpu.reciprocal(spread, approx=True)
    inverse = inverse * (2.0 - spread * inverse)
    value = jnp.maximum(near, 0.0) * jnp.maximum(away, 0.0) * (inverse * inverse)
    return value.astype(BF16)


def build_matrices(bands, geometry, landed, order, ids, kept, sides, wide):
    def widen(slot):
        record = landed[order(slot)].astype(F32)
        wide[slot, bands + 16 - record.shape[0] : bands + 16, :] = record
        ids[slot] = read_id(record[-1:])

    loop(wide.shape[0], widen)
    other_sides(bands, wide, sides)

    def build(slot):
        return form_factors(sides[slot], own_factors(geometry[jnp.maximum(ids[slot], 0)]))

    def keep(slot):
        kept[slot] = build(slot)

    loop(kept.shape[0], keep)
    return build


def first_sweep(bands, geometry, landed, order, ids, total, kept, sides, wide):
    build = build_matrices(bands, geometry, landed, order, ids, kept, sides, wide)

    def add(slot, matrix):
        own_id = ids[slot]
        weights = wide[slot, :bands, :].astype(BF16)
        terms = jnp.dot(weights, matrix, preferred_element_type=F32)
        total[jnp.maximum(own_id, 0)] += jnp.where(own_id >= 0, terms, 0.0)

    def add_kept(slot):
        add(slot, kept[slot])

    def add_built(slot):
        add(slot, build(slot))

    held, slots = kept.shape[0], wide.shape[0]
    loop(held, add_kept)
    if held < slots:
        lax.fori_loop(held, slots, lambda i, carry: (add_built(i), carry)[1], 0)


def column_kernel(bands, geometry, landed, total, kept, ids, sides, wide):
    total[...] = jnp.zeros_like(total)
    first_sweep(bands, geometry, landed, lambda i: i, ids, total, kept, sides, wide)


def other_column_kernel(bands, geometry, landed, after, kept, ids, sides, wide):
    build_matrices(bands, geometry, landed, lambda i: i, ids, kept, sides, wide)


def row_kernel(bands, cores, halves, geometry, landed, before, total, kept, ids, sides, wide):
    capacity = landed.shape[0] // (lax.axis_size("pairs") * halves)
    here = lax.axis_index("rep") // cores

    def order(slot):
        owner, back, entry = slot // (halves * capacity), slot // capacity % halves, slot % capacity
        half = lax.rem(here + (halves - back), halves)
        return (owner * halves + (halves - 1 - half)) * capacity + entry

    total[...] = before[...]
    first_sweep(bands, geometry, landed, order, ids, total, kept, sides, wide)


def add_kernel(parts, *refs):
    total = refs[0][...]
    for part in refs[1:parts]:
        total = total + part[...]
    refs[-1][...] = total


def weigh_kernel(halves, area, emission, reflect, mine, theirs, row_ids, *refs):
    col_ids = refs[:halves]
    sent, table = refs[halves:]
    radiosity = emission[...] + reflect[...] * (mine[...] + theirs[...])
    table[...] = area[...][:, None, :] * radiosity
    owners, twos = sent.shape[0], sent.shape[1]
    capacity = twos // halves

    def pick(owner, entry):
        if entry < twos:
            chosen = col_ids[entry // capacity][owner * capacity + entry % capacity]
        else:
            chosen = row_ids[owner * twos + entry - twos]
        return table[jnp.maximum(chosen, 0)]

    def one(owner):
        for two in range(twos):
            both = jnp.concatenate([pick(owner, 2 * two), pick(owner, 2 * two + 1)], axis=0)
            sent[owner, two] = both.astype(BF16)

    loop(owners, one)


def second_kernel(bands, halves, remade, landed, row_ids, row_kept, *refs):
    col_ids, col_kept = refs[:halves], refs[halves : 2 * halves]
    total = refs[-1]
    if remade:
        geometry, row_sides, *col_sides = refs[2 * halves : -1]
    total[...] = jnp.zeros_like(total)
    owners, twos = landed.shape[0], landed.shape[1]
    capacity = twos // halves

    def one(owner):
        for entry in range(2 * twos):
            part = entry // capacity - halves
            if entry < twos:
                ids, kept, slot = row_ids, row_kept, owner * twos + entry
            else:
                ids, kept = col_ids[part], col_kept[part]
                slot = owner * capacity + entry % capacity
            own_id = ids[slot]
            own = jnp.maximum(own_id, 0)
            weights = landed[owner, entry // 2]
            half = (entry % 2) * bands

            def add(matrix, own_id=own_id, own=own, weights=weights, half=half):
                terms = jnp.dot(weights, matrix, preferred_element_type=F32)
                total[own] += jnp.where(own_id >= 0, terms[half : half + bands], 0.0)

            if not remade:
                add(kept[slot])
                continue
            sides = row_sides if entry < twos else col_sides[part]

            def from_kept(slot=slot, kept=kept, add=add):
                add(kept[slot])

            def from_sides(slot=slot, own=own, sides=sides, add=add):
                add(form_factors(sides[slot], own_factors(geometry[own])))

            held = kept.shape[0]
            pl.when((own_id >= 0) & (slot < held))(from_kept)
            pl.when((own_id >= 0) & (slot >= held))(from_sides)

    loop(owners, one)


def in_hbm(x):
    return pltpu.with_memory_space_constraint(x, pltpu.HBM)


def in_smem(x):
    return pltpu.with_memory_space_constraint(x, pltpu.SMEM)


def call(kernel, outs, ins, out_specs, scratch=(), flops=0):
    sizes = [math.prod(s.shape) * s.dtype.itemsize for s in outs]
    held = [math.prod(s.shape) * s.dtype.itemsize for s in scratch if s.dtype in (F32, BF16)]
    room = 2 * sum(sizes) + sum(held) + 8 * 1024 * 1024
    return pl.pallas_call(
        kernel,
        out_shape=[
            spec.memory_space(s.shape, s.dtype) for s, spec in zip(outs, out_specs)
        ],
        in_specs=ins,
        out_specs=out_specs,
        scratch_shapes=scratch,
        compiler_params=pltpu.CompilerParams(vmem_limit_bytes=room),
        cost_estimate=pl.CostEstimate(flops=flops, bytes_accessed=sum(sizes), transcendentals=0),
    )


def shards(positions, facing, area, emission, reflect, pair_list):
    blocks, bands, patches = emission.shape
    owners = lax.axis_size("pairs")
    reps = lax.axis_size("rep")
    cores = 2 if reps % 2 == 0 else 1
    halves = reps // cores
    held = jnp.transpose(pair_list[0, 0], (1, 2, 0))
    capacity = held.shape[0]
    per_owner = halves * capacity
    slots = owners * per_owner
    near_slots = owners * capacity
    remade = slots > KEPT
    rows = bands + 16
    shape = jax.ShapeDtypeStruct
    total_shape = shape((blocks, bands, patches), F32)
    pair_flops = slots * patches * patches * 50

    def kept_of(count):
        return shape((min(count, KEPT), patches, patches), BF16)

    def sweep_room(count):
        sides = shape((count, DEPTH, patches), BF16)
        wide = pltpu.VMEM((count, rows + 8, patches), F32)
        if remade:
            return [sides], [wide]
        return [], [pltpu.VMEM(sides.shape, BF16), wide]

    table, geometry, sent, area, emission, reflect = call(
        functools.partial(stage_kernel, bands),
        [
            shape((blocks, rows, patches), F32),
            shape((blocks, 8, patches), F32),
            shape((owners, capacity, rows, patches), BF16),
            shape(area.shape, F32),
            total_shape,
            total_shape,
        ],
        [HBM] * 6,
        [VMEM] * 6,
        [
            pltpu.SMEM(held.shape, jnp.int32),
            pltpu.VMEM(positions.shape, F32),
            pltpu.VMEM(facing.shape, F32),
            pltpu.SemaphoreType.DMA((6,)),
        ],
    )(*[in_hbm(x) for x in (held, positions, facing, area, emission, reflect)])
    owner_order = [owner_at(place, owners) for place in range(owners)]

    def exchange(x):
        return lax.all_to_all(
            x,
            "pairs",
            split_axis=0,
            concat_axis=0,
            tiled=True,
            axis_index_groups=[owner_order],
        )

    landed = exchange(sent)
    col_side = landed.reshape(near_slots, rows, patches)
    sent, mirror = call(
        functools.partial(serve_kernel, halves),
        [
            shape((owners * halves, capacity, rows, patches), BF16),
            shape((near_slots, 16, patches), BF16),
        ],
        [VMEM, VMEM],
        [VMEM, VMEM],
    )(table, col_side)
    same_core = [
        [owner * reps + half * cores + core for owner in owner_order for half in reversed(range(halves))]
        for core in range(cores)
    ]
    landed = lax.all_to_all(
        sent,
        ("pairs", "rep"),
        split_axis=0,
        concat_axis=0,
        tiled=True,
        axis_index_groups=same_core,
    )
    row_side = landed.reshape(slots, rows, patches)

    def other_halves(x):
        return [
            lax.ppermute(x, "rep", [(i, (i + back * cores) % reps) for i in range(reps)])
            for back in range(1, halves)
        ]

    mirrors = other_halves(mirror)
    near_ids = shape((near_slots,), jnp.int32)
    outs, room = sweep_room(near_slots)
    col_total, kept, ids, *sides = call(
        functools.partial(column_kernel, bands),
        [total_shape, kept_of(near_slots), near_ids] + outs,
        [VMEM, VMEM],
        [VMEM, VMEM, SMEM] + [VMEM] * len(outs),
        room,
        pair_flops // halves,
    )(geometry, col_side)
    col_ids, col_kept, col_sides = [in_smem(ids)], [kept], [*sides]
    far_totals = other_halves(col_total)
    outs, room = sweep_room(slots)
    total, row_kept, row_ids, *row_sides = call(
        functools.partial(row_kernel, bands, cores, halves),
        [total_shape, kept_of(slots), shape((slots,), jnp.int32)] + outs,
        [VMEM, VMEM, VMEM],
        [VMEM, VMEM, SMEM] + [VMEM] * len(outs),
        room,
        pair_flops,
    )(geometry, row_side, col_total)
    row_ids = in_smem(row_ids)
    if far_totals:
        (total,) = call(
            functools.partial(add_kernel, halves),
            [total_shape],
            [VMEM] * (halves + len(mirrors)),
            [VMEM],
        )(total, *far_totals, *mirrors)
    outs, room = sweep_room(near_slots)
    for mirror in mirrors:
        kept, ids, *sides = call(
            functools.partial(other_column_kernel, bands),
            [kept_of(near_slots), near_ids] + outs,
            [VMEM, VMEM, VMEM],
            [VMEM, SMEM] + [VMEM] * len(outs),
            room,
            pair_flops // halves,
        )(geometry, mirror, total)
        col_ids.append(in_smem(ids))
        col_kept.append(kept)
        col_sides.extend(sides)

    def other_core(x):
        if cores == 1:
            return jnp.zeros_like(x)
        return lax.ppermute(x, "rep", [(i, i ^ 1) for i in range(reps)])

    (sent,) = call(
        functools.partial(weigh_kernel, halves),
        [shape((owners, per_owner, 2 * bands, patches), BF16)],
        [VMEM] * 5 + [SMEM] * (1 + halves),
        [VMEM],
        [pltpu.VMEM((blocks, bands, patches), F32)],
    )(area, emission, reflect, total, other_core(total), row_ids, *col_ids)
    landed = exchange(sent)
    extra = [geometry, *row_sides, *col_sides] if remade else []
    (total,) = call(
        functools.partial(second_kernel, bands, halves, remade),
        [total_shape],
        [VMEM, SMEM, VMEM] + [SMEM] * halves + [VMEM] * (halves + len(extra)),
        [VMEM],
        (),
        pair_flops,
    )(landed, row_ids, row_kept, *col_ids, *col_kept, *extra)
    return emission + reflect * (total + other_core(total))


def solution(mesh):
    placed = (
        P(None, "pairs", None),
        P(None, "pairs", None),
        P("pairs", None),
        P("pairs", None, None),
        P("pairs", None, None),
        P("pairs", "rep", None, None, None),
    )
    return jax.shard_map(
        shards, mesh=mesh, in_specs=placed, out_specs=P("pairs", None, None), check_vma=False
    )
```

```python
import functools
import math

import jax
import jax.numpy as jnp
from jax import lax
from jax.experimental import pallas as pl
from jax.experimental.pallas import tpu as pltpu
from jax.sharding import PartitionSpec as P

SOFTEN = 0.1
GROUP = 8
KEPT = 32
DEPTH = 48
F32 = jnp.float32
BF16 = jnp.bfloat16
VMEM = pl.BlockSpec(memory_space=pltpu.VMEM)
SMEM = pl.BlockSpec(memory_space=pltpu.SMEM)
HBM = pl.BlockSpec(memory_space=pltpu.HBM)


def loop(count, body):
    if count <= 16:
        for i in range(count):
            body(i)
    else:
        lax.fori_loop(0, count, lambda i, carry: (body(i), carry)[1], 0)


def owner_at(place, owners):
    first = owners // 2 + 1
    if owners & (owners - 1) == 0 and owners > 2:
        return place ^ first
    if isinstance(place, int):
        return (place + first) % owners
    return lax.rem(place + first, owners)


def pieces(value, count):
    parts = []
    for _ in range(count):
        part = value.astype(BF16).astype(F32)
        parts.append(part)
        value = value - part
    return parts


def dot_rows(a, b):
    return a[0] * b[0] + a[1] * b[1] + a[2] * b[2]


def with_ids(record, ids):
    rows = lax.broadcasted_iota(jnp.int32, record.shape, 0)
    return jnp.where(rows == record.shape[0] - 1, ids, record)


def read_id(ids):
    return ids[:, :128][0, 0].astype(jnp.int32)


def stage_kernel(
    bands,
    held_in,
    positions_in,
    facing_in,
    area_in,
    emission_in,
    reflect_in,
    table,
    geometry,
    sent,
    area,
    emission,
    reflect,
    held,
    positions,
    facing,
    done,
):
    moves = [
        pltpu.make_async_copy(src, dst, done.at[i])
        for i, (src, dst) in enumerate(
            (
                (facing_in, facing),
                (positions_in, positions),
                (area_in, area),
                (emission_in, emission),
                (held_in, held),
                (reflect_in, reflect),
            )
        )
    ]
    for move in moves:
        move.start()
    blocks, patches = area.shape
    capacity, _, owners = held.shape
    moves[0].wait()
    azimuth, elevation = facing[0], facing[1]
    level = jnp.cos(elevation)
    normal = [jnp.cos(azimuth) * level, jnp.sin(azimuth) * level, jnp.sin(elevation)]
    moves[1].wait()
    place = [positions[axis] for axis in range(3)]
    for axis in range(3):
        geometry[:, axis, :] = place[axis]
        geometry[:, 3 + axis, :] = normal[axis]
        high, middle, low = pieces(place[axis], 3)
        table[:, bands + axis, :] = high
        table[:, bands + 8 + axis, :] = middle
        table[:, bands + (6, 7, 14)[axis], :] = low
        high, low = pieces(normal[axis], 2)
        table[:, bands + 3 + axis, :] = high
        table[:, bands + 11 + axis, :] = low
    table[:, bands + 15, :] = jnp.zeros_like(azimuth)
    geometry[:, 6, :] = dot_rows(place, normal)
    geometry[:, 7, :] = dot_rows(place, place)
    moves[4].wait()
    lanes = lax.broadcasted_iota(jnp.int32, (1, patches), 1)
    moves[2].wait()
    moves[3].wait()
    table[:, :bands, :] = (area[...][:, None, :] * emission[...]).astype(BF16).astype(F32)

    def one(place):
        owner = owner_at(place, owners)
        for slot in range(capacity):
            row, col = held[slot, 0, owner], held[slot, 1, owner]
            filled = row >= 0
            row = jnp.where(filled, lax.rem(row, blocks), -1)
            col = jnp.where(filled, lax.rem(col, blocks), -1)
            ids = jnp.where(lanes < patches // 2, col.astype(F32), row.astype(F32))
            sent[place, slot] = with_ids(table[jnp.maximum(row, 0)], ids).astype(BF16)

    loop(owners, one)
    moves[5].wait()


def serve_kernel(copies, table, landed, sent, mirror):
    capacity = sent.shape[1]

    def one(slot):
        record = landed[slot].astype(F32)
        mirror[slot] = record[-16:].astype(BF16)
        ids = record[-1:]
        row = ids[:, ids.shape[1] // 2 :]
        answer = table[jnp.maximum(read_id(ids), 0)]
        answer = with_ids(answer, jnp.concatenate([row, row], axis=1)).astype(BF16)
        for copy in range(copies):
            sent[slot // capacity * copies + copy, slot % capacity] = answer

    loop(landed.shape[0], one)


def own_factors(tile):
    row = [tile[k : k + 1, :] for k in range(8)]
    none = jnp.zeros_like(row[0])
    unit = jnp.ones_like(none)

    def stack(*rows):
        return jnp.concatenate(rows, axis=0)

    n = list(zip(*[pieces(row[3 + k] * (1.0 / math.pi), 3) for k in range(3)]))
    c = pieces(row[6] * (-1.0 / math.pi), 3)
    near = stack(
        *n[0], none, none, none, n[0][0], n[0][1],
        *n[0], none, none, none, n[0][2], none,
        *n[1], none, none, none, none, none,
        *n[1], none, none, none, none, none,
        *n[2], none, none, none, c[0], c[1],
        none, none, none, none, none, none, c[2], none,
    )
    p = list(zip(*[pieces(row[k], 3) for k in range(3)]))
    away = stack(
        none, none, none, *p[0], none, none,
        none, none, none, *p[0], none, none,
        none, none, none, *p[1], none, none,
        none, none, none, *p[1], none, none,
        none, none, none, *p[2], none, none,
        -unit, -unit, -unit, none, none, none, none, none,
    )
    m = [[-2.0 * v for v in part] for part in p]
    e = pieces(row[7] + SOFTEN, 3)
    spread = stack(
        *m[0], none, none, none, m[0][0], m[0][1],
        *m[0], none, none, none, m[0][2], none,
        *m[1], none, none, none, none, none,
        *m[1], none, none, none, none, none,
        *m[2], none, none, none, e[0], e[1],
        none, none, none, unit, unit, unit, e[2], none,
    )
    return jnp.concatenate([near, away, spread], axis=1).astype(BF16)


def other_sides(bands, wide, sides):
    slots = wide.shape[0]

    def row(index):
        return wide[:, bands + index, :]

    place = [row(k) + row(8 + k) + row((6, 7, 14)[k]) for k in range(3)]
    normal = [row(3 + k) + row(11 + k) for k in range(3)]
    constants = pieces(dot_rows(place, normal), 3) + pieces(dot_rows(place, place), 3)
    constants += [jnp.ones_like(place[0]), jnp.zeros_like(place[0])]
    rows = lax.broadcasted_iota(jnp.int32, (8, wide.shape[2]), 0)
    for k, value in enumerate(constants):
        wide[:, bands + 16 + k, :] = value

    def side(slot):
        first = wide[slot, bands : bands + 8, :]
        second = wide[slot, bands + 8 : bands + 16, :]
        last = wide[slot, bands + 16 : bands + 24, :]
        with_ones = jnp.where(rows < 6, first, 1.0)
        sides[slot] = jnp.concatenate(
            [first, second, first, second, with_ones, last], axis=0
        ).astype(BF16)

    loop(slots, side)


def form_factors(side, factors):
    patches = side.shape[1]
    parts = lax.dot_general(
        side, factors, (((0,), (0,)), ((), ())), preferred_element_type=F32
    )
    near = parts[:, :patches]
    away = parts[:, patches : 2 * patches]
    spread = parts[:, 2 * patches :]
    inverse = pltpu.reciprocal(spread, approx=True)
    inverse = inverse * (2.0 - spread * inverse)
    value = jnp.maximum(near, 0.0) * jnp.maximum(away, 0.0) * (inverse * inverse)
    return value.astype(BF16)


def build_matrices(bands, geometry, landed, order, ids, kept, sides, wide):
    def widen(slot):
        record = landed[order(slot)].astype(F32)
        wide[slot, bands + 16 - record.shape[0] : bands + 16, :] = record
        ids[slot] = read_id(record[-1:])

    loop(wide.shape[0], widen)
    other_sides(bands, wide, sides)

    def build(slot):
        return form_factors(sides[slot], own_factors(geometry[jnp.maximum(ids[slot], 0)]))

    def keep(slot):
        kept[slot] = build(slot)

    return build, keep


def first_sweep(bands, geometry, landed, order, ids, total, kept, sides, wide):
    build, keep = build_matrices(bands, geometry, landed, order, ids, kept, sides, wide)

    def add(slot, matrix):
        own_id = ids[slot]
        weights = wide[slot, :bands, :].astype(BF16)
        terms = jnp.dot(weights, matrix, preferred_element_type=F32)
        total[jnp.maximum(own_id, 0)] += jnp.where(own_id >= 0, terms, 0.0)

    def add_kept(slot):
        add(slot, kept[slot])

    def add_built(slot):
        add(slot, build(slot))

    held, slots = kept.shape[0], wide.shape[0]
    for start in range(0, held, GROUP):
        count = min(GROUP, held - start)
        loop(count, lambda i: keep(start + i))
        loop(count, lambda i: add_kept(start + i))
    if held < slots:
        lax.fori_loop(held, slots, lambda i, carry: (add_built(i), carry)[1], 0)


def column_kernel(bands, geometry, landed, total, kept, ids, sides, wide):
    total[...] = jnp.zeros_like(total)
    first_sweep(bands, geometry, landed, lambda i: i, ids, total, kept, sides, wide)


def other_column_kernel(bands, geometry, landed, after, kept, ids, sides, wide):
    _, keep = build_matrices(bands, geometry, landed, lambda i: i, ids, kept, sides, wide)
    loop(kept.shape[0], keep)


def row_kernel(bands, cores, halves, geometry, landed, before, total, kept, ids, sides, wide):
    capacity = landed.shape[0] // (lax.axis_size("pairs") * halves)
    here = lax.axis_index("rep") // cores

    def order(slot):
        owner, back, entry = slot // (halves * capacity), slot // capacity % halves, slot % capacity
        half = lax.rem(here + (halves - back), halves)
        return (owner * halves + (halves - 1 - half)) * capacity + entry

    total[...] = before[...]
    first_sweep(bands, geometry, landed, order, ids, total, kept, sides, wide)


def add_kernel(parts, *refs):
    total = refs[0][...]
    for part in refs[1:parts]:
        total = total + part[...]
    refs[-1][...] = total


def weigh_kernel(halves, area, emission, reflect, mine, theirs, row_ids, *refs):
    col_ids = refs[:halves]
    sent, table = refs[halves:]
    radiosity = emission[...] + reflect[...] * (mine[...] + theirs[...])
    table[...] = area[...][:, None, :] * radiosity
    owners, twos = sent.shape[0], sent.shape[1]
    capacity = twos // halves

    def pick(owner, entry):
        if entry < twos:
            chosen = col_ids[entry // capacity][owner * capacity + entry % capacity]
        else:
            chosen = row_ids[owner * twos + entry - twos]
        return table[jnp.maximum(chosen, 0)]

    def one(owner):
        for two in range(twos):
            both = jnp.concatenate([pick(owner, 2 * two), pick(owner, 2 * two + 1)], axis=0)
            sent[owner, two] = both.astype(BF16)

    loop(owners, one)


def second_kernel(bands, halves, remade, landed, row_ids, row_kept, *refs):
    col_ids, col_kept = refs[:halves], refs[halves : 2 * halves]
    total = refs[-1]
    if remade:
        geometry, row_sides, *col_sides = refs[2 * halves : -1]
    total[...] = jnp.zeros_like(total)
    owners, twos = landed.shape[0], landed.shape[1]
    capacity = twos // halves

    def one(owner):
        for entry in range(2 * twos):
            part = entry // capacity - halves
            if entry < twos:
                ids, kept, slot = row_ids, row_kept, owner * twos + entry
            else:
                ids, kept = col_ids[part], col_kept[part]
                slot = owner * capacity + entry % capacity
            own_id = ids[slot]
            own = jnp.maximum(own_id, 0)
            weights = landed[owner, entry // 2]
            half = (entry % 2) * bands

            def add(matrix, own_id=own_id, own=own, weights=weights, half=half):
                terms = jnp.dot(weights, matrix, preferred_element_type=F32)
                total[own] += jnp.where(own_id >= 0, terms[half : half + bands], 0.0)

            if not remade:
                add(kept[slot])
                continue
            sides = row_sides if entry < twos else col_sides[part]

            def from_kept(slot=slot, kept=kept, add=add):
                add(kept[slot])

            def from_sides(slot=slot, own=own, sides=sides, add=add):
                add(form_factors(sides[slot], own_factors(geometry[own])))

            held = kept.shape[0]
            pl.when((own_id >= 0) & (slot < held))(from_kept)
            pl.when((own_id >= 0) & (slot >= held))(from_sides)

    loop(owners, one)


def in_hbm(x):
    return pltpu.with_memory_space_constraint(x, pltpu.HBM)


def in_smem(x):
    return pltpu.with_memory_space_constraint(x, pltpu.SMEM)


def call(kernel, outs, ins, out_specs, scratch=(), flops=0):
    sizes = [math.prod(s.shape) * s.dtype.itemsize for s in outs]
    held = [math.prod(s.shape) * s.dtype.itemsize for s in scratch if s.dtype in (F32, BF16)]
    room = 2 * sum(sizes) + sum(held) + 8 * 1024 * 1024
    return pl.pallas_call(
        kernel,
        out_shape=[
            spec.memory_space(s.shape, s.dtype) for s, spec in zip(outs, out_specs)
        ],
        in_specs=ins,
        out_specs=out_specs,
        scratch_shapes=scratch,
        compiler_params=pltpu.CompilerParams(vmem_limit_bytes=room),
        cost_estimate=pl.CostEstimate(flops=flops, bytes_accessed=sum(sizes), transcendentals=0),
    )


def shards(positions, facing, area, emission, reflect, pair_list):
    blocks, bands, patches = emission.shape
    owners = lax.axis_size("pairs")
    reps = lax.axis_size("rep")
    cores = 2 if reps % 2 == 0 else 1
    halves = reps // cores
    held = jnp.transpose(pair_list[0, 0], (1, 2, 0))
    capacity = held.shape[0]
    per_owner = halves * capacity
    slots = owners * per_owner
    near_slots = owners * capacity
    remade = slots > KEPT
    rows = bands + 16
    shape = jax.ShapeDtypeStruct
    total_shape = shape((blocks, bands, patches), F32)
    pair_flops = slots * patches * patches * 50

    def kept_of(count):
        return shape((min(count, KEPT), patches, patches), BF16)

    def sweep_room(count):
        sides = shape((count, DEPTH, patches), BF16)
        wide = pltpu.VMEM((count, rows + 8, patches), F32)
        if remade:
            return [sides], [wide]
        return [], [pltpu.VMEM(sides.shape, BF16), wide]

    table, geometry, sent, area, emission, reflect = call(
        functools.partial(stage_kernel, bands),
        [
            shape((blocks, rows, patches), F32),
            shape((blocks, 8, patches), F32),
            shape((owners, capacity, rows, patches), BF16),
            shape(area.shape, F32),
            total_shape,
            total_shape,
        ],
        [HBM] * 6,
        [VMEM] * 6,
        [
            pltpu.SMEM(held.shape, jnp.int32),
            pltpu.VMEM(positions.shape, F32),
            pltpu.VMEM(facing.shape, F32),
            pltpu.SemaphoreType.DMA((6,)),
        ],
    )(*[in_hbm(x) for x in (held, positions, facing, area, emission, reflect)])
    owner_order = [owner_at(place, owners) for place in range(owners)]

    def exchange(x):
        return lax.all_to_all(
            x,
            "pairs",
            split_axis=0,
            concat_axis=0,
            tiled=True,
            axis_index_groups=[owner_order],
        )

    landed = exchange(sent)
    col_side = landed.reshape(near_slots, rows, patches)
    sent, mirror = call(
        functools.partial(serve_kernel, halves),
        [
            shape((owners * halves, capacity, rows, patches), BF16),
            shape((near_slots, 16, patches), BF16),
        ],
        [VMEM, VMEM],
        [VMEM, VMEM],
    )(table, col_side)
    same_core = [
        [owner * reps + half * cores + core for owner in owner_order for half in reversed(range(halves))]
        for core in range(cores)
    ]
    landed = lax.all_to_all(
        sent,
        ("pairs", "rep"),
        split_axis=0,
        concat_axis=0,
        tiled=True,
        axis_index_groups=same_core,
    )
    row_side = landed.reshape(slots, rows, patches)

    def other_halves(x):
        return [
            lax.ppermute(x, "rep", [(i, (i + back * cores) % reps) for i in range(reps)])
            for back in range(1, halves)
        ]

    mirrors = other_halves(mirror)
    near_ids = shape((near_slots,), jnp.int32)
    outs, room = sweep_room(near_slots)
    col_total, kept, ids, *sides = call(
        functools.partial(column_kernel, bands),
        [total_shape, kept_of(near_slots), near_ids] + outs,
        [VMEM, VMEM],
        [VMEM, VMEM, SMEM] + [VMEM] * len(outs),
        room,
        pair_flops // halves,
    )(geometry, col_side)
    col_ids, col_kept, col_sides = [in_smem(ids)], [kept], [*sides]
    far_totals = other_halves(col_total)
    outs, room = sweep_room(slots)
    total, row_kept, row_ids, *row_sides = call(
        functools.partial(row_kernel, bands, cores, halves),
        [total_shape, kept_of(slots), shape((slots,), jnp.int32)] + outs,
        [VMEM, VMEM, VMEM],
        [VMEM, VMEM, SMEM] + [VMEM] * len(outs),
        room,
        pair_flops,
    )(geometry, row_side, col_total)
    row_ids = in_smem(row_ids)
    if far_totals:
        (total,) = call(
            functools.partial(add_kernel, halves),
            [total_shape],
            [VMEM] * (halves + len(mirrors)),
            [VMEM],
        )(total, *far_totals, *mirrors)
    outs, room = sweep_room(near_slots)
    for mirror in mirrors:
        kept, ids, *sides = call(
            functools.partial(other_column_kernel, bands),
            [kept_of(near_slots), near_ids] + outs,
            [VMEM, VMEM, VMEM],
            [VMEM, SMEM] + [VMEM] * len(outs),
            room,
            pair_flops // halves,
        )(geometry, mirror, total)
        col_ids.append(in_smem(ids))
        col_kept.append(kept)
        col_sides.extend(sides)

    def other_core(x):
        if cores == 1:
            return jnp.zeros_like(x)
        return lax.ppermute(x, "rep", [(i, i ^ 1) for i in range(reps)])

    (sent,) = call(
        functools.partial(weigh_kernel, halves),
        [shape((owners, per_owner, 2 * bands, patches), BF16)],
        [VMEM] * 5 + [SMEM] * (1 + halves),
        [VMEM],
        [pltpu.VMEM((blocks, bands, patches), F32)],
    )(area, emission, reflect, total, other_core(total), row_ids, *col_ids)
    landed = exchange(sent)
    extra = [geometry, *row_sides, *col_sides] if remade else []
    (total,) = call(
        functools.partial(second_kernel, bands, halves, remade),
        [total_shape],
        [VMEM, SMEM, VMEM] + [SMEM] * halves + [VMEM] * (halves + len(extra)),
        [VMEM],
        (),
        pair_flops,
    )(landed, row_ids, row_kept, *col_ids, *col_kept, *extra)
    return emission + reflect * (total + other_core(total))


def solution(mesh):
    placed = (
        P(None, "pairs", None),
        P(None, "pairs", None),
        P("pairs", None),
        P("pairs", None, None),
        P("pairs", None, None),
        P("pairs", "rep", None, None, None),
    )
    return jax.shard_map(
        shards, mesh=mesh, in_specs=placed, out_specs=P("pairs", None, None), check_vma=False
    )
```

```python
import functools
import math

import jax
import jax.numpy as jnp
from jax import lax
from jax.experimental import pallas as pl
from jax.experimental.pallas import tpu as pltpu
from jax.sharding import PartitionSpec as P

SOFTEN = 0.1
KEPT = 32
DEPTH = 48
F32 = jnp.float32
BF16 = jnp.bfloat16
VMEM = pl.BlockSpec(memory_space=pltpu.VMEM)
SMEM = pl.BlockSpec(memory_space=pltpu.SMEM)
HBM = pl.BlockSpec(memory_space=pltpu.HBM)


def loop(count, body):
    if count <= 16:
        for i in range(count):
            body(i)
    else:
        lax.fori_loop(0, count, lambda i, carry: (body(i), carry)[1], 0)


def owner_at(place, owners):
    first = owners // 2 + 1
    if owners & (owners - 1) == 0 and owners > 2:
        return (place * 3 + first) & (owners - 1)
    if isinstance(place, int):
        return (place + first) % owners
    return lax.rem(place + first, owners)


def pieces(value, count):
    parts = []
    for _ in range(count):
        part = value.astype(BF16).astype(F32)
        parts.append(part)
        value = value - part
    return parts


def dot_rows(a, b):
    return a[0] * b[0] + a[1] * b[1] + a[2] * b[2]


def with_ids(record, ids):
    rows = lax.broadcasted_iota(jnp.int32, record.shape, 0)
    return jnp.where(rows == record.shape[0] - 1, ids, record)


def read_id(ids):
    return ids[:, :128][0, 0].astype(jnp.int32)


def stage_kernel(
    bands,
    held_in,
    positions_in,
    facing_in,
    area_in,
    emission_in,
    reflect_in,
    table,
    geometry,
    sent,
    area,
    emission,
    reflect,
    held,
    positions,
    facing,
    done,
):
    moves = [
        pltpu.make_async_copy(src, dst, done.at[i])
        for i, (src, dst) in enumerate(
            (
                (facing_in, facing),
                (positions_in, positions),
                (area_in, area),
                (emission_in, emission),
                (held_in, held),
                (reflect_in, reflect),
            )
        )
    ]
    for move in moves:
        move.start()
    blocks, patches = area.shape
    capacity, _, owners = held.shape
    moves[0].wait()
    azimuth, elevation = facing[0], facing[1]
    level = jnp.cos(elevation)
    normal = [jnp.cos(azimuth) * level, jnp.sin(azimuth) * level, jnp.sin(elevation)]
    moves[1].wait()
    place = [positions[axis] for axis in range(3)]
    for axis in range(3):
        geometry[:, axis, :] = place[axis]
        geometry[:, 3 + axis, :] = normal[axis]
        high, middle, low = pieces(place[axis], 3)
        table[:, bands + axis, :] = high
        table[:, bands + 8 + axis, :] = middle
        table[:, bands + (6, 7, 14)[axis], :] = low
        high, low = pieces(normal[axis], 2)
        table[:, bands + 3 + axis, :] = high
        table[:, bands + 11 + axis, :] = low
    table[:, bands + 15, :] = jnp.zeros_like(azimuth)
    geometry[:, 6, :] = dot_rows(place, normal)
    geometry[:, 7, :] = dot_rows(place, place)
    moves[4].wait()
    lanes = lax.broadcasted_iota(jnp.int32, (1, patches), 1)
    moves[2].wait()
    moves[3].wait()
    table[:, :bands, :] = (area[...][:, None, :] * emission[...]).astype(BF16).astype(F32)

    def one(place):
        owner = owner_at(place, owners)
        for slot in range(capacity):
            row, col = held[slot, 0, owner], held[slot, 1, owner]
            filled = row >= 0
            row = jnp.where(filled, lax.rem(row, blocks), -1)
            col = jnp.where(filled, lax.rem(col, blocks), -1)
            ids = jnp.where(lanes < patches // 2, col.astype(F32), row.astype(F32))
            sent[place, slot] = with_ids(table[jnp.maximum(row, 0)], ids).astype(BF16)

    loop(owners, one)
    moves[5].wait()


def serve_kernel(copies, table, landed, sent, mirror):
    capacity = sent.shape[1]

    def one(slot):
        record = landed[slot].astype(F32)
        mirror[slot] = record[-16:].astype(BF16)
        ids = record[-1:]
        row = ids[:, ids.shape[1] // 2 :]
        answer = table[jnp.maximum(read_id(ids), 0)]
        answer = with_ids(answer, jnp.concatenate([row, row], axis=1)).astype(BF16)
        for copy in range(copies):
            sent[slot // capacity * copies + copy, slot % capacity] = answer

    loop(landed.shape[0], one)


def own_factors(tile):
    row = [tile[k : k + 1, :] for k in range(8)]
    none = jnp.zeros_like(row[0])
    unit = jnp.ones_like(none)

    def stack(*rows):
        return jnp.concatenate(rows, axis=0)

    n = list(zip(*[pieces(row[3 + k] * (1.0 / math.pi), 3) for k in range(3)]))
    c = pieces(row[6] * (-1.0 / math.pi), 3)
    near = stack(
        *n[0], none, none, none, n[0][0], n[0][1],
        *n[0], none, none, none, n[0][2], none,
        *n[1], none, none, none, none, none,
        *n[1], none, none, none, none, none,
        *n[2], none, none, none, c[0], c[1],
        none, none, none, none, none, none, c[2], none,
    )
    p = list(zip(*[pieces(row[k], 3) for k in range(3)]))
    away = stack(
        none, none, none, *p[0], none, none,
        none, none, none, *p[0], none, none,
        none, none, none, *p[1], none, none,
        none, none, none, *p[1], none, none,
        none, none, none, *p[2], none, none,
        -unit, -unit, -unit, none, none, none, none, none,
    )
    m = [[-2.0 * v for v in part] for part in p]
    e = pieces(row[7] + SOFTEN, 3)
    spread = stack(
        *m[0], none, none, none, m[0][0], m[0][1],
        *m[0], none, none, none, m[0][2], none,
        *m[1], none, none, none, none, none,
        *m[1], none, none, none, none, none,
        *m[2], none, none, none, e[0], e[1],
        none, none, none, unit, unit, unit, e[2], none,
    )
    return jnp.concatenate([near, away, spread], axis=1).astype(BF16)


def other_sides(bands, wide, sides):
    slots = wide.shape[0]

    def row(index):
        return wide[:, bands + index, :]

    place = [row(k) + row(8 + k) + row((6, 7, 14)[k]) for k in range(3)]
    normal = [row(3 + k) + row(11 + k) for k in range(3)]
    constants = pieces(dot_rows(place, normal), 3) + pieces(dot_rows(place, place), 3)
    constants += [jnp.ones_like(place[0]), jnp.zeros_like(place[0])]
    rows = lax.broadcasted_iota(jnp.int32, (8, wide.shape[2]), 0)
    for k, value in enumerate(constants):
        wide[:, bands + 16 + k, :] = value

    def side(slot):
        first = wide[slot, bands : bands + 8, :]
        second = wide[slot, bands + 8 : bands + 16, :]
        last = wide[slot, bands + 16 : bands + 24, :]
        with_ones = jnp.where(rows < 6, first, 1.0)
        sides[slot] = jnp.concatenate(
            [first, second, first, second, with_ones, last], axis=0
        ).astype(BF16)

    loop(slots, side)


def form_factors(side, factors):
    patches = side.shape[1]
    parts = lax.dot_general(
        side, factors, (((0,), (0,)), ((), ())), preferred_element_type=F32
    )
    near = parts[:, :patches]
    away = parts[:, patches : 2 * patches]
    spread = parts[:, 2 * patches :]
    inverse = pltpu.reciprocal(spread, approx=True)
    inverse = inverse * (2.0 - spread * inverse)
    value = jnp.maximum(near, 0.0) * jnp.maximum(away, 0.0) * (inverse * inverse)
    return value.astype(BF16)


def build_matrices(bands, geometry, landed, order, ids, kept, sides, wide):
    def widen(slot):
        record = landed[order(slot)].astype(F32)
        wide[slot, bands + 16 - record.shape[0] : bands + 16, :] = record
        ids[slot] = read_id(record[-1:])

    loop(wide.shape[0], widen)
    other_sides(bands, wide, sides)

    def build(slot):
        return form_factors(sides[slot], own_factors(geometry[jnp.maximum(ids[slot], 0)]))

    def keep(slot):
        kept[slot] = build(slot)

    loop(kept.shape[0], keep)
    return build


def first_sweep(bands, geometry, landed, order, ids, total, kept, sides, wide):
    build = build_matrices(bands, geometry, landed, order, ids, kept, sides, wide)

    def add(slot, matrix):
        own_id = ids[slot]
        weights = wide[slot, :bands, :].astype(BF16)
        terms = jnp.dot(weights, matrix, preferred_element_type=F32)
        total[jnp.maximum(own_id, 0)] += jnp.where(own_id >= 0, terms, 0.0)

    def add_kept(slot):
        add(slot, kept[slot])

    def add_built(slot):
        add(slot, build(slot))

    held, slots = kept.shape[0], wide.shape[0]
    loop(held, add_kept)
    if held < slots:
        lax.fori_loop(held, slots, lambda i, carry: (add_built(i), carry)[1], 0)


def column_kernel(bands, geometry, landed, total, kept, ids, sides, wide):
    total[...] = jnp.zeros_like(total)
    first_sweep(bands, geometry, landed, lambda i: i, ids, total, kept, sides, wide)


def other_column_kernel(bands, geometry, landed, after, kept, ids, sides, wide):
    build_matrices(bands, geometry, landed, lambda i: i, ids, kept, sides, wide)


def row_kernel(bands, cores, halves, geometry, landed, before, total, kept, ids, sides, wide):
    capacity = landed.shape[0] // (lax.axis_size("pairs") * halves)
    here = lax.axis_index("rep") // cores

    def order(slot):
        owner, back, entry = slot // (halves * capacity), slot // capacity % halves, slot % capacity
        half = lax.rem(here + (halves - back), halves)
        return (owner * halves + (halves - 1 - half)) * capacity + entry

    total[...] = before[...]
    first_sweep(bands, geometry, landed, order, ids, total, kept, sides, wide)


def add_kernel(parts, *refs):
    total = refs[0][...]
    for part in refs[1:parts]:
        total = total + part[...]
    refs[-1][...] = total


def weigh_kernel(halves, area, emission, reflect, mine, theirs, row_ids, *refs):
    col_ids = refs[:halves]
    sent, table = refs[halves:]
    radiosity = emission[...] + reflect[...] * (mine[...] + theirs[...])
    table[...] = area[...][:, None, :] * radiosity
    owners, twos = sent.shape[0], sent.shape[1]
    capacity = twos // halves

    def pick(owner, entry):
        if entry < twos:
            chosen = col_ids[entry // capacity][owner * capacity + entry % capacity]
        else:
            chosen = row_ids[owner * twos + entry - twos]
        return table[jnp.maximum(chosen, 0)]

    def one(owner):
        for two in range(twos):
            both = jnp.concatenate([pick(owner, 2 * two), pick(owner, 2 * two + 1)], axis=0)
            sent[owner, two] = both.astype(BF16)

    loop(owners, one)


def second_kernel(bands, halves, remade, landed, row_ids, row_kept, *refs):
    col_ids, col_kept = refs[:halves], refs[halves : 2 * halves]
    total = refs[-1]
    if remade:
        geometry, row_sides, *col_sides = refs[2 * halves : -1]
    total[...] = jnp.zeros_like(total)
    owners, twos = landed.shape[0], landed.shape[1]
    capacity = twos // halves

    def one(owner):
        for entry in range(2 * twos):
            part = entry // capacity - halves
            if entry < twos:
                ids, kept, slot = row_ids, row_kept, owner * twos + entry
            else:
                ids, kept = col_ids[part], col_kept[part]
                slot = owner * capacity + entry % capacity
            own_id = ids[slot]
            own = jnp.maximum(own_id, 0)
            weights = landed[owner, entry // 2]
            half = (entry % 2) * bands

            def add(matrix, own_id=own_id, own=own, weights=weights, half=half):
                terms = jnp.dot(weights, matrix, preferred_element_type=F32)
                total[own] += jnp.where(own_id >= 0, terms[half : half + bands], 0.0)

            if not remade:
                add(kept[slot])
                continue
            sides = row_sides if entry < twos else col_sides[part]

            def from_kept(slot=slot, kept=kept, add=add):
                add(kept[slot])

            def from_sides(slot=slot, own=own, sides=sides, add=add):
                add(form_factors(sides[slot], own_factors(geometry[own])))

            held = kept.shape[0]
            pl.when((own_id >= 0) & (slot < held))(from_kept)
            pl.when((own_id >= 0) & (slot >= held))(from_sides)

    loop(owners, one)


def in_hbm(x):
    return pltpu.with_memory_space_constraint(x, pltpu.HBM)


def in_smem(x):
    return pltpu.with_memory_space_constraint(x, pltpu.SMEM)


def call(kernel, outs, ins, out_specs, scratch=(), flops=0):
    sizes = [math.prod(s.shape) * s.dtype.itemsize for s in outs]
    held = [math.prod(s.shape) * s.dtype.itemsize for s in scratch if s.dtype in (F32, BF16)]
    room = 2 * sum(sizes) + sum(held) + 8 * 1024 * 1024
    return pl.pallas_call(
        kernel,
        out_shape=[
            spec.memory_space(s.shape, s.dtype) for s, spec in zip(outs, out_specs)
        ],
        in_specs=ins,
        out_specs=out_specs,
        scratch_shapes=scratch,
        compiler_params=pltpu.CompilerParams(vmem_limit_bytes=room),
        cost_estimate=pl.CostEstimate(flops=flops, bytes_accessed=sum(sizes), transcendentals=0),
    )


def shards(positions, facing, area, emission, reflect, pair_list):
    blocks, bands, patches = emission.shape
    owners = lax.axis_size("pairs")
    reps = lax.axis_size("rep")
    cores = 2 if reps % 2 == 0 else 1
    halves = reps // cores
    held = jnp.transpose(pair_list[0, 0], (1, 2, 0))
    capacity = held.shape[0]
    per_owner = halves * capacity
    slots = owners * per_owner
    near_slots = owners * capacity
    remade = slots > KEPT
    rows = bands + 16
    shape = jax.ShapeDtypeStruct
    total_shape = shape((blocks, bands, patches), F32)
    pair_flops = slots * patches * patches * 50

    def kept_of(count):
        return shape((min(count, KEPT), patches, patches), BF16)

    def sweep_room(count):
        sides = shape((count, DEPTH, patches), BF16)
        wide = pltpu.VMEM((count, rows + 8, patches), F32)
        if remade:
            return [sides], [wide]
        return [], [pltpu.VMEM(sides.shape, BF16), wide]

    table, geometry, sent, area, emission, reflect = call(
        functools.partial(stage_kernel, bands),
        [
            shape((blocks, rows, patches), F32),
            shape((blocks, 8, patches), F32),
            shape((owners, capacity, rows, patches), BF16),
            shape(area.shape, F32),
            total_shape,
            total_shape,
        ],
        [HBM] * 6,
        [VMEM] * 6,
        [
            pltpu.SMEM(held.shape, jnp.int32),
            pltpu.VMEM(positions.shape, F32),
            pltpu.VMEM(facing.shape, F32),
            pltpu.SemaphoreType.DMA((6,)),
        ],
    )(*[in_hbm(x) for x in (held, positions, facing, area, emission, reflect)])
    owner_order = [owner_at(place, owners) for place in range(owners)]

    def exchange(x):
        return lax.all_to_all(
            x,
            "pairs",
            split_axis=0,
            concat_axis=0,
            tiled=True,
            axis_index_groups=[owner_order],
        )

    landed = exchange(sent)
    col_side = landed.reshape(near_slots, rows, patches)
    sent, mirror = call(
        functools.partial(serve_kernel, halves),
        [
            shape((owners * halves, capacity, rows, patches), BF16),
            shape((near_slots, 16, patches), BF16),
        ],
        [VMEM, VMEM],
        [VMEM, VMEM],
    )(table, col_side)
    same_core = [
        [owner * reps + half * cores + core for owner in owner_order for half in reversed(range(halves))]
        for core in range(cores)
    ]
    landed = lax.all_to_all(
        sent,
        ("pairs", "rep"),
        split_axis=0,
        concat_axis=0,
        tiled=True,
        axis_index_groups=same_core,
    )
    row_side = landed.reshape(slots, rows, patches)

    def other_halves(x):
        return [
            lax.ppermute(x, "rep", [(i, (i + back * cores) % reps) for i in range(reps)])
            for back in range(1, halves)
        ]

    mirrors = other_halves(mirror)
    near_ids = shape((near_slots,), jnp.int32)
    outs, room = sweep_room(near_slots)
    col_total, kept, ids, *sides = call(
        functools.partial(column_kernel, bands),
        [total_shape, kept_of(near_slots), near_ids] + outs,
        [VMEM, VMEM],
        [VMEM, VMEM, SMEM] + [VMEM] * len(outs),
        room,
        pair_flops // halves,
    )(geometry, col_side)
    col_ids, col_kept, col_sides = [in_smem(ids)], [kept], [*sides]
    far_totals = other_halves(col_total)
    outs, room = sweep_room(slots)
    total, row_kept, row_ids, *row_sides = call(
        functools.partial(row_kernel, bands, cores, halves),
        [total_shape, kept_of(slots), shape((slots,), jnp.int32)] + outs,
        [VMEM, VMEM, VMEM],
        [VMEM, VMEM, SMEM] + [VMEM] * len(outs),
        room,
        pair_flops,
    )(geometry, row_side, col_total)
    row_ids = in_smem(row_ids)
    if far_totals:
        (total,) = call(
            functools.partial(add_kernel, halves),
            [total_shape],
            [VMEM] * (halves + len(mirrors)),
            [VMEM],
        )(total, *far_totals, *mirrors)
    outs, room = sweep_room(near_slots)
    for mirror in mirrors:
        kept, ids, *sides = call(
            functools.partial(other_column_kernel, bands),
            [kept_of(near_slots), near_ids] + outs,
            [VMEM, VMEM, VMEM],
            [VMEM, SMEM] + [VMEM] * len(outs),
            room,
            pair_flops // halves,
        )(geometry, mirror, total)
        col_ids.append(in_smem(ids))
        col_kept.append(kept)
        col_sides.extend(sides)

    def other_core(x):
        if cores == 1:
            return jnp.zeros_like(x)
        return lax.ppermute(x, "rep", [(i, i ^ 1) for i in range(reps)])

    (sent,) = call(
        functools.partial(weigh_kernel, halves),
        [shape((owners, per_owner, 2 * bands, patches), BF16)],
        [VMEM] * 5 + [SMEM] * (1 + halves),
        [VMEM],
        [pltpu.VMEM((blocks, bands, patches), F32)],
    )(area, emission, reflect, total, other_core(total), row_ids, *col_ids)
    landed = exchange(sent)
    extra = [geometry, *row_sides, *col_sides] if remade else []
    (total,) = call(
        functools.partial(second_kernel, bands, halves, remade),
        [total_shape],
        [VMEM, SMEM, VMEM] + [SMEM] * halves + [VMEM] * (halves + len(extra)),
        [VMEM],
        (),
        pair_flops,
    )(landed, row_ids, row_kept, *col_ids, *col_kept, *extra)
    return emission + reflect * (total + other_core(total))


def solution(mesh):
    placed = (
        P(None, "pairs", None),
        P(None, "pairs", None),
        P("pairs", None),
        P("pairs", None, None),
        P("pairs", None, None),
        P("pairs", "rep", None, None, None),
    )
    return jax.shard_map(
        shards, mesh=mesh, in_specs=placed, out_specs=P("pairs", None, None), check_vma=False
    )
```
